32 devices in a mesh: leaf: 8 (over y, x, core), blk: 4 (over z).
Axes of the slice: x: 2, y: 2, z: 4, core: 2. Of those that a mesh axis runs over, the one named last changes fastest.
Arguments:
- interface: bfloat16 [32768, 512], P(('leaf', 'blk')), may hold values from -6 to 6
- owners: int32 [32768, 1], P(('leaf', 'blk')), may hold values from 0 to 7; in each aligned block of 1024 rows (0 to 1023, 1024 to 2047, ...) at most 256 rows name the same one
- keep_proj: bfloat16 [3, 512, 512], replicated, may hold values from -0.25 to 0.25
- sibling_proj: bfloat16 [3, 512, 512], replicated, may hold values from -0.25 to 0.25
- coupling: bfloat16 [8, 512, 512], P('leaf'), may hold values from -0.25 to 0.25
- pattern: int32 [8, 8, 8], P('leaf'), may hold values 0 or 1
Outputs:
- coupled: bfloat16 [32768, 512], P(('leaf', 'blk'))
The draws below stay inside these ranges and needn't reach their ends.
Inputs may be any that keep to these rules, and one draw needn't show every extreme that they name: `owners`: among the 1024 rows of one device no owner is named by more than 256 rows, a bound that some block reaches.
All inputs are finite; a program needn't handle non-finite values. No bound on the sum of `pattern` on one device may be relied on, other than what follows from the above.
Results may differ from the reference program's by a relative error of at most 0.0075.
Values may be sent and summed in bfloat16 or wider, within the bound.
No kernel may reach another device: no remote copies, remote signals or barrier semaphores. Data moves between devices by JAX's collectives and lax.ppermute only.
A program may use at most 64 MiB of HBM per device.

```python
import math
import jax
import jax.numpy as jnp
import numpy as np
from jax import lax

MODES = 512
BS = 64
LEVELS = 3
ROWS = 1024
NBLK = 8
TOTAL = 32768
N_LEAF = 8
N_BLK = 4


def place_ends(entries, stream_key, low, high):
    dims = entries.shape
    index_at = [jax.random.randint(jax.random.fold_in(stream_key, axis), (), 0, dims[axis]) for axis in range(len(dims))]
    entries = entries.at[tuple(index_at)].set(low)
    longest = dims.index(max(dims))
    index_at[longest] = (index_at[longest] + 1) % dims[longest]
    return entries.at[tuple(index_at)].set(high)


def shard_levels(rng, extent, pieces, low, high):
    gain = 1.0
    for dim, shards_of in pieces:
        heights = jax.random.uniform(jax.random.fold_in(jax.random.fold_in(rng, 6), dim), (shards_of,), jnp.float32, low / len(pieces), high / len(pieces))
        gain = gain * jnp.repeat(jnp.exp(heights), extent[dim] // shards_of).reshape((-1,) + (1,) * (len(extent) - 1 - dim))
    return gain


def assign_block(own_key, own, number, rows, count, top, bound, lean):
    ranking = jax.random.permutation(own_key, count)
    crowded, usual = load_shares(count, rows * top, bound, lean, True), load_shares(count, rows * top, bound, lean, False)
    places = jnp.arange(count)

    def named(lengths, rotation):
        used = int((lengths > 0).sum())
        fixed = max(1, used // 4)
        passed = fixed + (places - fixed + rotation * (used - fixed)) % max(1, count - fixed)
        return jnp.zeros((count,), jnp.int32).at[ranking[jnp.where(places < fixed, places, passed)]].set(jnp.asarray(lengths, jnp.int32))

    lengths = jnp.where(number % 4 == 0, named(crowded, number // 4), named(usual, number - number // 4 - 1))
    mixed = jax.random.permutation(jax.random.fold_in(own, 3), count)
    source_of, taker = mixed[0:count // 2 * 2:2], mixed[1:count // 2 * 2:2]
    margin = jnp.minimum(lengths[source_of] - 1, bound - lengths[taker]) // 2
    margin = jnp.where((source_of == ranking[0]) | (taker == ranking[0]) | (lengths[taker] == 0), 0, jnp.maximum(margin, 0))
    passed = jax.random.randint(jax.random.fold_in(own, 4), (count // 2,), 0, 1 << 20) % (margin + 1)
    lengths = lengths.at[source_of].add(-passed).at[taker].add(passed)
    items = jnp.searchsorted(jnp.cumsum(lengths), jnp.arange(rows * top), side="right").astype(jnp.int32)
    listing = items.reshape(top, rows).T
    listing = listing[jax.random.permutation(jax.random.fold_in(own, 1), rows)]
    rotation = jax.random.randint(jax.random.fold_in(own, 2), (rows, 1), 0, top)
    return jnp.take_along_axis(listing, (jnp.arange(top)[None, :] + rotation) % top, axis=1)


def load_shares(amount, total, most, slope, full):
    weights = [(1 << 20) // math.isqrt(grade ** slope) + 1 for grade in range(1, amount + 1)]
    largest = most if full else min(most, max(-(-total // amount), total * weights[0] // sum(weights)))
    least = 1 if total - largest >= amount - 1 else 0
    holding, spare = [largest] + [least] * (amount - 1), total - largest - least * (amount - 1)
    while spare > 0:
        candidates = [i for i in range(1, amount) if holding[i] < largest] or [i for i in range(1, amount) if holding[i] < most]
        pool, budget = sum([weights[i] for i in candidates]), spare
        for i in candidates:
            addition = min(most - holding[i], max(1, budget * weights[i] // pool), spare)
            holding[i] = holding[i] + addition
            spare = spare - addition
    return np.array(holding)


def noise(own_key, extent, spread, bound, pieces=(), kind=jnp.bfloat16):
    level = shard_levels(own_key, extent, pieces, -0.22, 0.18) if pieces else 1.0
    array = jax.random.normal(own_key, extent, jnp.float32) * spread * level
    return jnp.minimum(jnp.maximum(array, -bound), bound).astype(kind)


def setup_inputs(seed: int = 0) -> dict:
    arg_keys = jax.random.split(jax.random.key(seed), 7)
    interface = noise(arg_keys[0], (TOTAL, MODES), 1.0, 6.0, ((0, 32),))
    owners_keys = jax.random.split(jax.random.fold_in(arg_keys[1], 1), TOTAL // ROWS)
    owners_turns = jax.random.permutation(jax.random.fold_in(arg_keys[1], 3), TOTAL // ROWS)
    owners = jax.vmap(lambda own, number: assign_block(jax.random.fold_in(arg_keys[1], 2), own, number, ROWS, N_LEAF, 1, 2 * ROWS // N_LEAF, 2))(owners_keys, owners_turns).reshape((TOTAL, 1))
    keep_proj = noise(arg_keys[2], (LEVELS, MODES, MODES), MODES ** -0.5, 0.25)
    sibling_proj = noise(arg_keys[3], (LEVELS, MODES, MODES), MODES ** -0.5, 0.25)
    coupling = noise(arg_keys[4], (N_LEAF, MODES, MODES), MODES ** -0.5, 0.25, ((0, 8),))
    pattern = place_ends((jax.random.randint(arg_keys[5], (N_LEAF, NBLK, NBLK), 0, 2) < 1).astype(jnp.int32), jax.random.fold_in(arg_keys[5], 1), 0, 1)
    return dict(interface=interface, owners=owners, keep_proj=keep_proj, sibling_proj=sibling_proj, coupling=coupling, pattern=pattern)


epsilon = 1e-06

def expand_mask(mask_block):
    return jnp.repeat(jnp.repeat(mask_block, BS, axis=0), BS, axis=1)

def reference(interface, owners, keep_proj, sibling_proj, coupling, pattern):
    current = interface
    for tree_level in range(LEVELS):
        blocked = current.reshape(N_LEAF, N_BLK * ROWS, MODES)
        partner = np.arange(N_LEAF) ^ 1 << tree_level
        sibling = blocked[partner].reshape(-1, MODES)
        combined = jnp.dot(current, keep_proj[tree_level], preferred_element_type=jnp.float32)
        combined = combined + jnp.dot(sibling, sibling_proj[tree_level], preferred_element_type=jnp.float32)
        scale_rows = lax.rsqrt(lax.optimization_barrier(jnp.mean(combined * combined, axis=1, keepdims=True)) + epsilon)
        current = (combined * scale_rows).astype(jnp.bfloat16)
    capacity = 2 * ROWS // N_LEAF
    target = owners[:, 0].reshape(N_LEAF * N_BLK, ROWS).astype(jnp.int32)
    onehot = (target[:, :, None] == jnp.arange(N_LEAF, dtype=jnp.int32)[None, None, :]).astype(jnp.int32)
    slot_index = (lax.optimization_barrier(jnp.sum(jnp.cumsum(onehot, axis=1) * onehot, axis=2)) - 1).astype(jnp.int32)
    position = (target * capacity + slot_index).astype(jnp.int32)
    source = current.reshape(N_LEAF * N_BLK, ROWS, MODES)

    def fill_rows(rows_in, where):
        return jnp.zeros((N_LEAF * capacity, MODES), current.dtype).at[where].set(rows_in)
    outgoing = jax.vmap(fill_rows)(source, position)
    outgoing = outgoing.reshape(N_LEAF, N_BLK, N_LEAF, capacity, MODES).transpose(2, 1, 0, 3, 4)

    def apply_owner(operands):
        block_rows, weight, mask_block = operands
        dense = weight * expand_mask(mask_block).astype(weight.dtype)
        product = jnp.dot(block_rows.reshape(-1, MODES), dense, preferred_element_type=jnp.float32)
        return product.astype(jnp.bfloat16).reshape(block_rows.shape)
    coupled = lax.map(apply_owner, (outgoing, coupling, pattern))
    returned = coupled.transpose(2, 1, 0, 3, 4).reshape(N_LEAF * N_BLK, N_LEAF * capacity, MODES)
    result = jax.vmap(lambda rows_in, where: rows_in[where])(returned, position)
    return result.reshape(-1, MODES)
```

```python
import functools
import jax
import jax.numpy as jnp
from jax import lax
from jax.experimental import pallas as pl
from jax.experimental.pallas import tpu as pltpu
from jax.sharding import PartitionSpec as P

BS = 64
LEVELS = 3
EPSILON = 1e-06
VMEM = pl.BlockSpec(memory_space=pltpu.VMEM)
SMEM = pl.BlockSpec(memory_space=pltpu.SMEM)


def swapped(value, mask):
    pairs = [(source, source ^ mask) for source in range(lax.axis_size("leaf"))]
    return lax.ppermute(value, "leaf", pairs)


def mixed(own, sibling, keep, cross):
    combined = jnp.dot(own, keep, preferred_element_type=jnp.float32)
    combined = combined + jnp.dot(sibling, cross, preferred_element_type=jnp.float32)
    scale_rows = lax.rsqrt(jnp.mean(combined * combined, axis=1, keepdims=True) + EPSILON)
    return (combined * scale_rows).astype(jnp.bfloat16)


def call(body, outs, cost, n_smem, *args):
    return pl.pallas_call(
        body,
        out_shape=outs,
        in_specs=[SMEM] * n_smem + [VMEM] * (len(args) - n_smem),
        out_specs=jax.tree.map(lambda _: VMEM, outs),
        cost_estimate=pl.CostEstimate(flops=cost, bytes_accessed=4 << 20, transcendentals=0),
        compiler_params=pltpu.CompilerParams(vmem_limit_bytes=40 << 20),
    )(*args)


def first_level(chip, own, sibling, keep, cross, *outs):
    size = outs[0].shape[0]
    for m, out in enumerate(outs):
        rows = pl.ds(pl.multiple_of((chip[0] ^ m) * size, size), size)
        out[...] = mixed(own[rows, :], sibling[rows, :], keep[...], cross[...])


def later_levels(x0, x1, x2, x3, keep, cross, *outs):
    current = [x0[...], x1[...], x2[...], x3[...]]
    current = [mixed(current[m], current[m ^ 1], keep[1], cross[1]) for m in range(4)]
    for m in range(4):
        outs[m][...] = mixed(current[m], current[m ^ 2], keep[2], cross[2])


def masked_coupling(coupling, pattern, out):
    for i in range(pattern.shape[1]):
        row = jnp.concatenate(
            [jnp.full((BS, BS), pattern[0, i, j], jnp.int32) for j in range(pattern.shape[2])], axis=1
        )
        block = coupling[0, i * BS : (i + 1) * BS, :]
        out[i * BS : (i + 1) * BS, :] = jnp.where(row != 0, block, jnp.zeros_like(block))


def couple(n_owner, me, owners, x0, x1, x2, x3, *rest):
    dense, out = rest[:n_owner], rest[n_owner]
    size = x0.shape[0]
    for m, x in enumerate((x0, x1, x2, x3)):
        rows = pl.ds(pl.multiple_of(((me[0] >> 1) ^ m) * size, size), size)
        relative = owners[rows, :] ^ me[0]
        total = jnp.zeros(x.shape, jnp.float32)
        value = x[...]
        for o in range(n_owner):
            chosen = jnp.where(relative == o, value, jnp.zeros_like(value))
            total += jnp.dot(chosen, dense[o][...], preferred_element_type=jnp.float32)
        out[rows, :] = total.astype(jnp.bfloat16)


def gathered_coupling(dense):
    across = [dense] + [swapped(dense, 2 * m) for m in range(1, 4)]
    return [each for mine in across for each in (mine, swapped(mine, 1))]


def routed(current, owners, dense):
    row_count, features = current.shape
    leaves = lax.axis_size("leaf")
    capacity = 2 * row_count // leaves
    target = owners[:, 0]
    onehot = (target[:, None] == jnp.arange(leaves, dtype=jnp.int32)[None, :]).astype(jnp.int32)
    slot_index = jnp.sum(jnp.cumsum(onehot, axis=0) * onehot, axis=1) - 1
    position = target * capacity + slot_index
    outgoing = jnp.zeros((leaves * capacity, features), jnp.bfloat16).at[position].set(current)
    sectioned = outgoing.reshape(leaves, capacity, features)
    arrived = lax.all_to_all(sectioned, "leaf", split_axis=0, concat_axis=0, tiled=True)
    product = jnp.einsum("...m,mn->...n", arrived, dense, preferred_element_type=jnp.float32)
    result = product.astype(jnp.bfloat16)
    returned = lax.all_to_all(result, "leaf", split_axis=0, concat_axis=0, tiled=True)
    return returned.reshape(leaves * capacity, features)[position]


def local(interface, owners, keep_proj, sibling_proj, coupling, pattern):
    rows, features = interface.shape
    leaves = lax.axis_size("leaf")
    me = lax.axis_index("leaf").astype(jnp.int32)
    quarter = rows // 4
    work = 4 * rows * features * features
    part = jax.ShapeDtypeStruct((quarter, features), jnp.bfloat16)
    chip = (me // 2 % 4).reshape(1)

    sibling = swapped(interface, 1)
    dense = call(
        masked_coupling, jax.ShapeDtypeStruct(coupling.shape[1:], jnp.bfloat16), 0, 0, coupling, pattern
    )
    few = leaves == 8
    if few:
        matrices = gathered_coupling(dense)
    sent = call(first_level, [part] * 4, work, 1, chip, interface, sibling, keep_proj[0], sibling_proj[0])
    mixed_rows = [sent[0]] + [swapped(sent[m], 2 * m) for m in range(1, 4)]
    done = call(later_levels, [part] * 4, 2 * work, 0, *mixed_rows, keep_proj, sibling_proj)
    back = [done[0]] + [swapped(done[m], 2 * m) for m in range(1, 4)]
    if few:
        return call(
            functools.partial(couple, leaves),
            jax.ShapeDtypeStruct((rows, features), jnp.bfloat16),
            2 * work,
            1,
            me.reshape(1),
            owners,
            *back,
            *matrices,
        )
    current = jnp.zeros((rows, features), jnp.bfloat16)
    for m in range(4):
        current = lax.dynamic_update_slice_in_dim(current, back[m], (chip[0] ^ m) * quarter, 0)
    return routed(current, owners, dense)


def solution(mesh):
    in_specs = (
        P(("leaf", "blk"), None),
        P(("leaf", "blk"), None),
        P(),
        P(),
        P("leaf", None, None),
        P("leaf", None, None),
    )
    out_specs = P(("leaf", "blk"), None)
    return jax.shard_map(local, mesh=mesh, in_specs=in_specs, out_specs=out_specs, check_vma=False)
```

```python
import functools
import jax
import jax.numpy as jnp
from jax import lax
from jax.experimental import pallas as pl
from jax.experimental.pallas import tpu as pltpu
from jax.sharding import PartitionSpec as P

BS = 64
EPSILON = 1e-06
VMEM = pl.BlockSpec(memory_space=pltpu.VMEM)
SMEM = pl.BlockSpec(memory_space=pltpu.SMEM)
HBM = pl.BlockSpec(memory_space=pltpu.HBM)


def swapped(value, mask, axis="leaf"):
    pairs = [(source, source ^ mask) for source in range(lax.axis_size(axis))]
    return lax.ppermute(value, axis, pairs)


def in_hbm(value):
    return pltpu.with_memory_space_constraint(value, pltpu.HBM)


def together(*values):
    return lax.optimization_barrier(values)


def after(value, *others):
    return lax.optimization_barrier((value, *others))[0]


def mixed(own, sibling, keep, cross):
    combined = jnp.dot(own, keep, preferred_element_type=jnp.float32)
    combined = combined + jnp.dot(sibling, cross, preferred_element_type=jnp.float32)
    scale_rows = lax.rsqrt(jnp.mean(combined * combined, axis=1, keepdims=True) + EPSILON)
    return (combined * scale_rows).astype(jnp.bfloat16)


def call(body, outs, flops, specs, *args, scratch=(), aliases=None):
    return pl.pallas_call(
        body,
        out_shape=[shape for shape, _ in outs],
        in_specs=specs,
        out_specs=[spec for _, spec in outs],
        scratch_shapes=list(scratch),
        input_output_aliases=aliases or {},
        cost_estimate=pl.CostEstimate(flops=flops, bytes_accessed=flops // 512, transcendentals=0),
        compiler_params=pltpu.CompilerParams(vmem_limit_bytes=24 << 20),
    )(*args)


def block_rows(me, m, size):
    return pl.ds(pl.multiple_of((((me[0] >> 1) & 3) ^ m) * size, size), size)


def first_level(me, sibling, interface, keep, cross, *rest):
    outs, (own, keep_here, cross_here, sems) = rest[:4], rest[4:]
    size = outs[0].shape[0]
    loads = [
        pltpu.make_async_copy(keep.at[0], keep_here, sems.at[4]),
        pltpu.make_async_copy(cross.at[0], cross_here, sems.at[5]),
    ]
    order = (1, 2, 3, 0)
    for m in order:
        rows = block_rows(me, m, size)
        loads.append(pltpu.make_async_copy(interface.at[rows], own.at[rows], sems.at[m]))
    for load in loads:
        load.start()
    loads[0].wait()
    loads[1].wait()
    for m, load in zip(order, loads[2:]):
        load.wait()
        rows = block_rows(me, m, size)
        outs[m][...] = mixed(own[rows, :], sibling[rows, :], keep_here[...], cross_here[...])


def second_level(x0, x1, keep, cross, out0, out1):
    out0[...] = mixed(x0[...], x1[...], keep[0], cross[0])
    out1[...] = mixed(x1[...], x0[...], keep[0], cross[0])


def third_level(x2, x3, y0, y1, keep, cross, *outs):
    y2 = mixed(x2[...], x3[...], keep[0], cross[0])
    y3 = mixed(x3[...], x2[...], keep[0], cross[0])
    outs[1][...] = mixed(y1[...], y3, keep[1], cross[1])
    outs[2][...] = mixed(y2, y0[...], keep[1], cross[1])
    outs[3][...] = mixed(y3, y1[...], keep[1], cross[1])
    outs[0][...] = mixed(y0[...], y2, keep[1], cross[1])


def masked_coupling(z, coupling, pattern, out, part, held, shown, sems):
    loads = [pltpu.make_async_copy(pattern, shown, sems.at[0]), pltpu.make_async_copy(coupling, held, sems.at[1])]
    for load in loads:
        load.start()
    for load in loads:
        load.wait()
    for i in range(shown.shape[1]):
        row = jnp.concatenate(
            [jnp.full((BS, BS), shown[0, i, j], jnp.int32) for j in range(shown.shape[2])], axis=1
        )
        block = held[0, i * BS : (i + 1) * BS, :]
        out[i * BS : (i + 1) * BS, :] = jnp.where(row != 0, block, jnp.zeros_like(block))
    part[...] = out[half_rows(z, 0, part.shape[0]), :]


def half_rows(z, other, depth):
    return pl.ds(pl.multiple_of(((z[0] & 1) ^ other) * depth, depth), depth)


def packed(*refs):
    *parts, out = refs
    at = 0
    for part in parts:
        out[at : at + part.shape[0], :] = part[...]
        at += part.shape[0]


def couple(m, me, z, owners, x, own, beside, *rest):
    packs, (out, held, sems) = rest[:2], rest[-3:]
    size, features = x.shape
    depth = features // 2
    rows = block_rows(me, m, size)
    lanes = owners.shape[1]
    groups = size // lanes
    diagonal = lax.broadcasted_iota(jnp.int32, (lanes, lanes), 0) == lax.broadcasted_iota(jnp.int32, (lanes, lanes), 1)
    named = owners[pl.ds((((me[0] >> 1) & 3) ^ m) * groups, groups), :] ^ me[0]
    relative = jnp.concatenate(
        [jnp.sum(jnp.where(diagonal, named[i : i + 1, :], 0), axis=1, keepdims=True) for i in range(groups)], axis=0
    )
    parts = [half_rows(z, other, depth) for other in range(2)]
    values = [x[:, part] for part in parts]
    chosen = [[jnp.where(relative == r, value, jnp.zeros_like(value)) for value in values] for r in range(8)]
    copies = []
    for n in range(2):
        columns = slice(n * depth, (n + 1) * depth)
        total = jnp.zeros((size, depth), jnp.float32)
        for r in range(8):
            for h in range(2):
                if r < 2:
                    piece = (own, beside)[r][parts[h], columns]
                else:
                    at = (r // 2 - 1 + 3 * h) * depth
                    piece = packs[r % 2][at : at + depth, columns]
                total += jnp.dot(chosen[r][h], piece, preferred_element_type=jnp.float32)
        held[:, columns] = total.astype(jnp.bfloat16)
        copies.append(pltpu.make_async_copy(held.at[:, columns], out.at[rows, columns], sems.at[n]))
        copies[-1].start()
    for copy in copies:
        copy.wait()


def fetched(keep, cross, keep_here, cross_here, sems):
    loads = [
        pltpu.make_async_copy(keep.at[1:], keep_here, sems.at[0]),
        pltpu.make_async_copy(cross.at[1:], cross_here, sems.at[1]),
    ]
    for load in loads:
        load.start()
    for load in loads:
        load.wait()


def routed(current, owners, dense):
    row_count, features = current.shape
    leaves = lax.axis_size("leaf")
    capacity = 2 * row_count // leaves
    target = owners[:, 0]
    onehot = (target[:, None] == jnp.arange(leaves, dtype=jnp.int32)[None, :]).astype(jnp.int32)
    slot_index = jnp.sum(jnp.cumsum(onehot, axis=0) * onehot, axis=1) - 1
    position = target * capacity + slot_index
    outgoing = jnp.zeros((leaves * capacity, features), jnp.bfloat16).at[position].set(current)
    sectioned = outgoing.reshape(leaves, capacity, features)
    arrived = lax.all_to_all(sectioned, "leaf", split_axis=0, concat_axis=0, tiled=True)
    product = jnp.einsum("...m,mn->...n", arrived, dense, preferred_element_type=jnp.float32)
    result = product.astype(jnp.bfloat16)
    returned = lax.all_to_all(result, "leaf", split_axis=0, concat_axis=0, tiled=True)
    return returned.reshape(leaves * capacity, features)[position]


def local(interface, owners, keep_proj, sibling_proj, coupling, pattern):
    rows, features = interface.shape
    leaves = lax.axis_size("leaf")
    me = lax.axis_index("leaf").astype(jnp.int32).reshape(1)
    z = lax.axis_index("blk").astype(jnp.int32).reshape(1)
    few = leaves == 8 and lax.axis_size("blk") % 2 == 0
    quarter = rows // 4
    depth = features // 2
    block_flops = 2 * quarter * features * features

    def array(*shape, space=VMEM):
        return jax.ShapeDtypeStruct(shape, jnp.bfloat16), space

    part = array(quarter, features)
    whole = array(rows, features, space=HBM)
    matrix = array(features, features)
    weights = in_hbm(keep_proj), in_hbm(sibling_proj)

    sibling = swapped(interface, 1)
    dense, mine = call(
        masked_coupling,
        [matrix, array(depth, features)],
        1,
        [SMEM] + [HBM] * 2,
        z,
        in_hbm(coupling),
        in_hbm(pattern),
        scratch=[
            pltpu.VMEM(coupling.shape, coupling.dtype),
            pltpu.VMEM(pattern.shape, pattern.dtype),
            pltpu.SemaphoreType.DMA((2,)),
        ],
    )
    if few:
        near = swapped(mine, 2), swapped(mine, 4)
        beside = swapped(dense, 1)
        sibling = after(sibling, beside)
    sent = call(
        first_level,
        [part] * 4,
        4 * block_flops,
        [SMEM, VMEM] + [HBM] * 3,
        me,
        sibling,
        in_hbm(interface),
        *weights,
        scratch=[pltpu.VMEM((rows, features), jnp.bfloat16)]
        + [pltpu.VMEM((features, features), jnp.bfloat16)] * 2
        + [pltpu.SemaphoreType.DMA((6,))],
    )
    x = [sent[0]] + [swapped(sent[m], 2 * m) for m in (1, 2, 3)]
    weights = call(
        fetched,
        [array(2, features, features)] * 2,
        1,
        [HBM] * 2,
        *(in_hbm(w) for w in together(keep_proj, sibling_proj, sent[0])[:2]),
        scratch=[pltpu.SemaphoreType.DMA((2,))],
    )
    if few:
        x_mine, y_mine, _ = together(*near, sent[0])
        x_other, y_other = swapped(x_mine, 1, "blk"), swapped(y_mine, 1, "blk")
        d_mine, d_other = swapped(y_mine, 2), swapped(x_other, 4)
        x = together(*x)
    y0, y1 = call(second_level, [part] * 2, (1 << 34), [VMEM] * 4, x[0], x[1], *weights)
    done = call(third_level, [part] * 4, (1 << 34), [VMEM] * 6, x[2], x[3], y0, y1, *weights)
    back = [done[0]] + [swapped(done[m], 2 * m) for m in (1, 2, 3)]
    if not few:
        current = jnp.zeros((rows, features), jnp.bfloat16)
        for m in range(4):
            current = lax.dynamic_update_slice_in_dim(current, back[m], ((me[0] // 2 % 4) ^ m) * quarter, 0)
        return routed(current, owners, dense)
    pieces = [x_mine, y_mine, d_mine, x_other, y_other, d_other]
    (pack,) = call(packed, [array(6 * depth, features)], 1, [VMEM] * 6, *together(*pieces, done[0])[:6])
    matrices = [dense, beside, pack, swapped(pack, 1)]
    out = None
    for m in range(4):
        extra = [] if out is None else [out]
        (out,) = call(
            functools.partial(couple, m),
            [whole],
            8 * block_flops,
            [SMEM] * 2 + [VMEM] * (2 + len(matrices)) + [HBM] * len(extra),
            me,
            z,
            owners.reshape(-1, 128),
            back[m],
            *matrices,
            *extra,
            scratch=[pltpu.VMEM((quarter, features), jnp.bfloat16), pltpu.SemaphoreType.DMA((2,))],
            aliases={4 + len(matrices): 0} if extra else None,
        )
    return out


def solution(mesh):
    in_specs = (
        P(("leaf", "blk"), None),
        P(("leaf", "blk"), None),
        P(),
        P(),
        P("leaf", None, None),
        P("leaf", None, None),
    )
    out_specs = P(("leaf", "blk"), None)
    return jax.shard_map(local, mesh=mesh, in_specs=in_specs, out_specs=out_specs, check_vma=False)
```

```python
import functools
import jax
import jax.numpy as jnp
from jax import lax
from jax.experimental import pallas as pl
from jax.experimental.pallas import tpu as pltpu
from jax.sharding import PartitionSpec as P

BS = 64
EPSILON = 1e-06
PLACES = (0, 1), (2, 4), (5, 3), (6, 7)
VMEM = pl.BlockSpec(memory_space=pltpu.VMEM)
SMEM = pl.BlockSpec(memory_space=pltpu.SMEM)
HBM = pl.BlockSpec(memory_space=pltpu.HBM)


def swapped(value, mask, axis="leaf"):
    pairs = [(source, source ^ mask) for source in range(lax.axis_size(axis))]
    return lax.ppermute(value, axis, pairs)


def in_hbm(value):
    return pltpu.with_memory_space_constraint(value, pltpu.HBM)


def together(*values):
    return lax.optimization_barrier(values)


def after(value, *others):
    return lax.optimization_barrier((value, *others))[0]


def mixed(own, sibling, keep, cross):
    combined = jnp.dot(own, keep, preferred_element_type=jnp.float32)
    combined = combined + jnp.dot(sibling, cross, preferred_element_type=jnp.float32)
    scale_rows = lax.rsqrt(jnp.mean(combined * combined, axis=1, keepdims=True) + EPSILON)
    return (combined * scale_rows).astype(jnp.bfloat16)


def call(body, outs, flops, specs, *args, scratch=(), aliases=None):
    return pl.pallas_call(
        body,
        out_shape=[shape for shape, _ in outs],
        in_specs=specs,
        out_specs=[spec for _, spec in outs],
        scratch_shapes=list(scratch),
        input_output_aliases=aliases or {},
        cost_estimate=pl.CostEstimate(flops=flops, bytes_accessed=flops // 512, transcendentals=0),
        compiler_params=pltpu.CompilerParams(vmem_limit_bytes=24 << 20),
    )(*args)


def block_rows(me, m, size):
    return pl.ds(pl.multiple_of((((me[0] >> 1) & 3) ^ m) * size, size), size)


def first_level(me, sibling, interface, keep, cross, *rest):
    outs, (own, keep_here, cross_here, sems) = rest[:4], rest[4:]
    size = outs[0].shape[0]
    loads = [
        pltpu.make_async_copy(keep.at[0], keep_here, sems.at[4]),
        pltpu.make_async_copy(cross.at[0], cross_here, sems.at[5]),
    ]
    order = (1, 2, 3, 0)
    for m in order:
        rows = block_rows(me, m, size)
        loads.append(pltpu.make_async_copy(interface.at[rows], own.at[rows], sems.at[m]))
    for load in loads:
        load.start()
    loads[0].wait()
    loads[1].wait()
    for m, load in zip(order, loads[2:]):
        load.wait()
        rows = block_rows(me, m, size)
        outs[m][...] = mixed(own[rows, :], sibling[rows, :], keep_here[...], cross_here[...])


def second_level(x0, x1, keep, cross, out0, out1):
    out0[...] = mixed(x0[...], x1[...], keep[0], cross[0])
    out1[...] = mixed(x1[...], x0[...], keep[0], cross[0])


def third_level(x2, x3, y0, y1, keep, cross, *outs):
    y2 = mixed(x2[...], x3[...], keep[0], cross[0])
    y3 = mixed(x3[...], x2[...], keep[0], cross[0])
    outs[1][...] = mixed(y1[...], y3, keep[1], cross[1])
    outs[2][...] = mixed(y2, y0[...], keep[1], cross[1])
    outs[3][...] = mixed(y3, y1[...], keep[1], cross[1])
    outs[0][...] = mixed(y0[...], y2, keep[1], cross[1])


def masked_coupling(z, coupling, pattern, part, rest, held, shown, sems):
    loads = [pltpu.make_async_copy(pattern, shown, sems.at[0]), pltpu.make_async_copy(coupling, held, sems.at[1])]
    for load in loads:
        load.start()
    for load in loads:
        load.wait()
    for i in range(shown.shape[1]):
        row = jnp.concatenate(
            [jnp.full((BS, BS), shown[0, i, j], jnp.int32) for j in range(shown.shape[2])], axis=1
        )
        block = held[0, i * BS : (i + 1) * BS, :]
        held[0, i * BS : (i + 1) * BS, :] = jnp.where(row != 0, block, jnp.zeros_like(block))
    part[...] = held[0, half_rows(z, 0, part.shape[0]), :]
    rest[...] = held[0, half_rows(z, 1, part.shape[0]), :]


def half_rows(z, other, depth):
    return pl.ds(pl.multiple_of(((z[0] & 1) ^ other) * depth, depth), depth)


def packed(*refs):
    *parts, out = refs
    at = 0
    for part in parts:
        out[at : at + part.shape[0], :] = part[...]
        at += part.shape[0]


def couple(blocks, me, z, owners, *rest):
    n_block = len(blocks)
    xs, packs, (out, held, sems) = rest[:n_block], rest[n_block : n_block + 2], rest[-3:]
    size, features = xs[0].shape
    depth = features // 2
    lanes = owners.shape[1]
    groups = size // lanes
    diagonal = lax.broadcasted_iota(jnp.int32, (lanes, lanes), 0) == lax.broadcasted_iota(jnp.int32, (lanes, lanes), 1)
    columns_of = []
    for m in blocks:
        named = owners[pl.ds((((me[0] >> 1) & 3) ^ m) * groups, groups), :] ^ me[0]
        columns_of += [jnp.sum(jnp.where(diagonal, named[i : i + 1, :], 0), axis=1, keepdims=True) for i in range(groups)]
    relative = jnp.concatenate(columns_of, axis=0)
    parts = [half_rows(z, other, depth) for other in range(2)]
    values = [jnp.concatenate([x[:, part] for x in xs], axis=0) for part in parts]
    chosen = [[jnp.where(relative == r, value, jnp.zeros_like(value)) for value in values] for r in range(8)]
    copies = []
    for n in range(2):
        columns = slice(n * depth, (n + 1) * depth)
        total = jnp.zeros((n_block * size, depth), jnp.float32)
        for r in range(8):
            for h in range(2):
                at = PLACES[r // 2][h] * depth
                piece = packs[r % 2][at : at + depth, columns]
                total += jnp.dot(chosen[r][h], piece, preferred_element_type=jnp.float32)
        held[:, columns] = total.astype(jnp.bfloat16)
        for i, m in enumerate(blocks):
            to = out.at[block_rows(me, m, size), columns]
            copies.append(pltpu.make_async_copy(held.at[i * size : (i + 1) * size, columns], to, sems.at[n, i]))
            copies[-1].start()
    for copy in copies:
        copy.wait()


def fetched(keep, cross, keep_here, cross_here, sems):
    loads = [
        pltpu.make_async_copy(keep.at[1:], keep_here, sems.at[0]),
        pltpu.make_async_copy(cross.at[1:], cross_here, sems.at[1]),
    ]
    for load in loads:
        load.start()
    for load in loads:
        load.wait()


def routed(current, owners, dense):
    row_count, features = current.shape
    leaves = lax.axis_size("leaf")
    capacity = 2 * row_count // leaves
    target = owners[:, 0]
    onehot = (target[:, None] == jnp.arange(leaves, dtype=jnp.int32)[None, :]).astype(jnp.int32)
    slot_index = jnp.sum(jnp.cumsum(onehot, axis=0) * onehot, axis=1) - 1
    position = target * capacity + slot_index
    outgoing = jnp.zeros((leaves * capacity, features), jnp.bfloat16).at[position].set(current)
    sectioned = outgoing.reshape(leaves, capacity, features)
    arrived = lax.all_to_all(sectioned, "leaf", split_axis=0, concat_axis=0, tiled=True)
    product = jnp.einsum("...m,mn->...n", arrived, dense, preferred_element_type=jnp.float32)
    result = product.astype(jnp.bfloat16)
    returned = lax.all_to_all(result, "leaf", split_axis=0, concat_axis=0, tiled=True)
    return returned.reshape(leaves * capacity, features)[position]


def local(interface, owners, keep_proj, sibling_proj, coupling, pattern):
    rows, features = interface.shape
    leaves = lax.axis_size("leaf")
    me = lax.axis_index("leaf").astype(jnp.int32).reshape(1)
    z = lax.axis_index("blk").astype(jnp.int32).reshape(1)
    few = leaves == 8 and lax.axis_size("blk") % 2 == 0
    quarter = rows // 4
    depth = features // 2
    block_flops = 2 * quarter * features * features

    def array(*shape, space=VMEM):
        return jax.ShapeDtypeStruct(shape, jnp.bfloat16), space

    part = array(quarter, features)
    whole = array(rows, features, space=HBM)
    matrix = array(features, features)
    weights = in_hbm(keep_proj), in_hbm(sibling_proj)

    sibling = swapped(interface, 1)
    mine, other = call(
        masked_coupling,
        [array(depth, features)] * 2,
        1,
        [SMEM] + [HBM] * 2,
        z,
        in_hbm(coupling),
        in_hbm(pattern),
        scratch=[
            pltpu.VMEM(coupling.shape, coupling.dtype),
            pltpu.VMEM(pattern.shape, pattern.dtype),
            pltpu.SemaphoreType.DMA((2,)),
        ],
    )
    if few:
        near = swapped(mine, 2), swapped(other, 4)
    sent = call(
        first_level,
        [part] * 4,
        4 * block_flops,
        [SMEM, VMEM] + [HBM] * 3,
        me,
        sibling,
        in_hbm(interface),
        *weights,
        scratch=[pltpu.VMEM((rows, features), jnp.bfloat16)]
        + [pltpu.VMEM((features, features), jnp.bfloat16)] * 2
        + [pltpu.SemaphoreType.DMA((6,))],
    )
    x = [sent[0]] + [swapped(sent[m], 2 * m) for m in (1, 2, 3)]
    weights = call(
        fetched,
        [array(2, features, features)] * 2,
        1,
        [HBM] * 2,
        *(in_hbm(w) for w in together(keep_proj, sibling_proj, sent[0])[:2]),
        scratch=[pltpu.SemaphoreType.DMA((2,))],
    )
    if few:
        x_mine, y_other, _ = together(*near, sent[0])
        (pack_near,) = call(packed, [array(2 * depth, features)], 1, [VMEM] * 2, x_mine, y_other)
        pack_far = swapped(pack_near, 1, "blk")
        d_mine, d_other = swapped(after(x_mine, x[1]), 4), swapped(after(y_other, x[1]), 2)
        x = together(*x)
    y0, y1 = call(second_level, [part] * 2, (1 << 34), [VMEM] * 4, x[0], x[1], *weights)
    done = call(third_level, [part] * 4, (1 << 34), [VMEM] * 6, x[2], x[3], y0, y1, *weights)
    back = [done[0]] + [swapped(done[m], 2 * m) for m in (1, 2, 3)]
    if not few:
        current = jnp.zeros((rows, features), jnp.bfloat16)
        for m in range(4):
            current = lax.dynamic_update_slice_in_dim(current, back[m], ((me[0] // 2 % 4) ^ m) * quarter, 0)
        return routed(current, owners, jnp.where(z[0] % 2 == 0, jnp.concatenate([mine, other]), jnp.concatenate([other, mine])))
    pieces = [mine, other, pack_near, pack_far, d_mine, d_other]
    (pack,) = call(packed, [array(8 * depth, features)], 1, [VMEM] * 6, *together(*pieces, done[0])[:6])
    matrices = [pack, swapped(pack, 1)]
    out = None
    for blocks in ((0, 1), (2, 3)):
        extra = [] if out is None else [out]
        n_block = len(blocks)
        (out,) = call(
            functools.partial(couple, blocks),
            [whole],
            8 * n_block * block_flops,
            [SMEM] * 2 + [VMEM] * (1 + n_block + len(matrices)) + [HBM] * len(extra),
            me,
            z,
            owners.reshape(-1, 128),
            *(back[m] for m in blocks),
            *matrices,
            *extra,
            scratch=[pltpu.VMEM((n_block * quarter, features), jnp.bfloat16), pltpu.SemaphoreType.DMA((2, n_block))],
            aliases={3 + n_block + len(matrices): 0} if extra else None,
        )
    return out


def solution(mesh):
    in_specs = (
        P(("leaf", "blk"), None),
        P(("leaf", "blk"), None),
        P(),
        P(),
        P("leaf", None, None),
        P("leaf", None, None),
    )
    out_specs = P(("leaf", "blk"), None)
    return jax.shard_map(local, mesh=mesh, in_specs=in_specs, out_specs=out_specs, check_vma=False)
```

```python
import functools
import jax
import jax.numpy as jnp
from jax import lax
from jax.experimental import pallas as pl
from jax.experimental.pallas import tpu as pltpu
from jax.sharding import PartitionSpec as P

BS = 64
EPSILON = 1e-06
PLACES = (0, 1), (2, 4), (5, 3), (6, 7)
VMEM = pl.BlockSpec(memory_space=pltpu.VMEM)
SMEM = pl.BlockSpec(memory_space=pltpu.SMEM)
HBM = pl.BlockSpec(memory_space=pltpu.HBM)


def swapped(value, mask, axis="leaf"):
    pairs = [(source, source ^ mask) for source in range(lax.axis_size(axis))]
    return lax.ppermute(value, axis, pairs)


def in_hbm(value):
    return pltpu.with_memory_space_constraint(value, pltpu.HBM)


def together(*values):
    return lax.optimization_barrier(values)


def after(value, *others):
    return lax.optimization_barrier((value, *others))[0]


def mixed(own, sibling, keep, cross):
    combined = jnp.dot(own, keep, preferred_element_type=jnp.float32)
    combined = combined + jnp.dot(sibling, cross, preferred_element_type=jnp.float32)
    scale_rows = lax.rsqrt(jnp.mean(combined * combined, axis=1, keepdims=True) + EPSILON)
    return (combined * scale_rows).astype(jnp.bfloat16)


def call(body, outs, flops, specs, *args, scratch=(), aliases=None):
    return pl.pallas_call(
        body,
        out_shape=[shape for shape, _ in outs],
        in_specs=specs,
        out_specs=[spec for _, spec in outs],
        scratch_shapes=list(scratch),
        input_output_aliases=aliases or {},
        cost_estimate=pl.CostEstimate(flops=flops, bytes_accessed=flops // 512, transcendentals=0),
        compiler_params=pltpu.CompilerParams(vmem_limit_bytes=24 << 20),
    )(*args)


def block_rows(me, m, size):
    return pl.ds(pl.multiple_of((((me[0] >> 1) & 3) ^ m) * size, size), size)


def first_level(me, sibling, interface, keep, cross, *rest):
    outs, (own, keep_here, cross_here, sems) = rest[:4], rest[4:]
    size = outs[0].shape[0]
    loads = [
        pltpu.make_async_copy(keep.at[0], keep_here, sems.at[4]),
        pltpu.make_async_copy(cross.at[0], cross_here, sems.at[5]),
    ]
    order = (1, 2, 3, 0)
    for m in order:
        rows = block_rows(me, m, size)
        loads.append(pltpu.make_async_copy(interface.at[rows], own.at[rows], sems.at[m]))
    for load in loads:
        load.start()
    loads[0].wait()
    loads[1].wait()
    for m, load in zip(order, loads[2:]):
        load.wait()
        rows = block_rows(me, m, size)
        outs[m][...] = mixed(own[rows, :], sibling[rows, :], keep_here[...], cross_here[...])


def second_level(x0, x1, keep, cross, out0, out1):
    out0[...] = mixed(x0[...], x1[...], keep[0], cross[0])
    out1[...] = mixed(x1[...], x0[...], keep[0], cross[0])


def third_level(x2, x3, y0, y1, keep, cross, *outs):
    y2 = mixed(x2[...], x3[...], keep[0], cross[0])
    y3 = mixed(x3[...], x2[...], keep[0], cross[0])
    outs[1][...] = mixed(y1[...], y3, keep[1], cross[1])
    outs[2][...] = mixed(y2, y0[...], keep[1], cross[1])
    outs[3][...] = mixed(y3, y1[...], keep[1], cross[1])
    outs[0][...] = mixed(y0[...], y2, keep[1], cross[1])


def masked_coupling(z, coupling, pattern, part, rest, held, shown, sems):
    loads = [pltpu.make_async_copy(pattern, shown, sems.at[0]), pltpu.make_async_copy(coupling, held, sems.at[1])]
    for load in loads:
        load.start()
    for load in loads:
        load.wait()
    for i in range(shown.shape[1]):
        row = jnp.concatenate(
            [jnp.full((BS, BS), shown[0, i, j], jnp.int32) for j in range(shown.shape[2])], axis=1
        )
        block = held[0, i * BS : (i + 1) * BS, :]
        held[0, i * BS : (i + 1) * BS, :] = jnp.where(row != 0, block, jnp.zeros_like(block))
    part[...] = held[0, half_rows(z, 0, part.shape[0]), :]
    rest[...] = held[0, half_rows(z, 1, part.shape[0]), :]


def half_rows(z, other, depth):
    return pl.ds(pl.multiple_of(((z[0] & 1) ^ other) * depth, depth), depth)


def packed(*refs):
    *parts, out = refs
    at = 0
    for part in parts:
        out[at : at + part.shape[0], :] = part[...]
        at += part.shape[0]


def couple(blocks, me, z, owners, *rest):
    n_block = len(blocks)
    xs, packs, (out, held, sems) = rest[:n_block], rest[n_block : n_block + 2], rest[-3:]
    size, features = xs[0].shape
    depth = features // 2
    lanes = owners.shape[1]
    groups = size // lanes
    diagonal = lax.broadcasted_iota(jnp.int32, (lanes, lanes), 0) == lax.broadcasted_iota(jnp.int32, (lanes, lanes), 1)
    columns_of = []
    for m in blocks:
        named = owners[pl.ds((((me[0] >> 1) & 3) ^ m) * groups, groups), :] ^ me[0]
        columns_of += [jnp.sum(jnp.where(diagonal, named[i : i + 1, :], 0), axis=1, keepdims=True) for i in range(groups)]
    relative = jnp.concatenate(columns_of, axis=0)
    parts = [half_rows(z, other, depth) for other in range(2)]
    values = [jnp.concatenate([x[:, part] for x in xs], axis=0) for part in parts]
    chosen = [[jnp.where(relative == r, value, jnp.zeros_like(value)) for value in values] for r in range(8)]
    copies = []
    for n in range(2):
        columns = slice(n * depth, (n + 1) * depth)
        total = jnp.zeros((n_block * size, depth), jnp.float32)
        for r in range(8):
            for h in range(2):
                at = PLACES[r // 2][h] * depth
                piece = packs[r % 2][at : at + depth, columns]
                total += jnp.dot(chosen[r][h], piece, preferred_element_type=jnp.float32)
        held[:, columns] = total.astype(jnp.bfloat16)
        for i, m in enumerate(blocks):
            to = out.at[block_rows(me, m, size), columns]
            copies.append(pltpu.make_async_copy(held.at[i * size : (i + 1) * size, columns], to, sems.at[n, i]))
            copies[-1].start()
    for copy in copies:
        copy.wait()


def passed(*refs):
    count = len(refs) // 2
    for value, out in zip(refs[:count], refs[count:]):
        out[...] = value[...]


def fetched(keep, cross, keep_here, cross_here, sems):
    loads = [
        pltpu.make_async_copy(keep.at[1:], keep_here, sems.at[0]),
        pltpu.make_async_copy(cross.at[1:], cross_here, sems.at[1]),
    ]
    for load in loads:
        load.start()
    for load in loads:
        load.wait()


def routed(current, owners, dense):
    row_count, features = current.shape
    leaves = lax.axis_size("leaf")
    capacity = 2 * row_count // leaves
    target = owners[:, 0]
    onehot = (target[:, None] == jnp.arange(leaves, dtype=jnp.int32)[None, :]).astype(jnp.int32)
    slot_index = jnp.sum(jnp.cumsum(onehot, axis=0) * onehot, axis=1) - 1
    position = target * capacity + slot_index
    outgoing = jnp.zeros((leaves * capacity, features), jnp.bfloat16).at[position].set(current)
    sectioned = outgoing.reshape(leaves, capacity, features)
    arrived = lax.all_to_all(sectioned, "leaf", split_axis=0, concat_axis=0, tiled=True)
    product = jnp.einsum("...m,mn->...n", arrived, dense, preferred_element_type=jnp.float32)
    result = product.astype(jnp.bfloat16)
    returned = lax.all_to_all(result, "leaf", split_axis=0, concat_axis=0, tiled=True)
    return returned.reshape(leaves * capacity, features)[position]


def local(interface, owners, keep_proj, sibling_proj, coupling, pattern):
    rows, features = interface.shape
    leaves = lax.axis_size("leaf")
    me = lax.axis_index("leaf").astype(jnp.int32).reshape(1)
    z = lax.axis_index("blk").astype(jnp.int32).reshape(1)
    few = leaves == 8 and lax.axis_size("blk") % 2 == 0
    quarter = rows // 4
    depth = features // 2
    block_flops = 2 * quarter * features * features

    def array(*shape, space=VMEM):
        return jax.ShapeDtypeStruct(shape, jnp.bfloat16), space

    part = array(quarter, features)
    whole = array(rows, features, space=HBM)
    matrix = array(features, features)
    weights = in_hbm(keep_proj), in_hbm(sibling_proj)

    sibling = swapped(interface, 1)
    mine, other = call(
        masked_coupling,
        [array(depth, features)] * 2,
        1,
        [SMEM] + [HBM] * 2,
        z,
        in_hbm(coupling),
        in_hbm(pattern),
        scratch=[
            pltpu.VMEM(coupling.shape, coupling.dtype),
            pltpu.VMEM(pattern.shape, pattern.dtype),
            pltpu.SemaphoreType.DMA((2,)),
        ],
    )
    if few:
        near = swapped(mine, 2), swapped(other, 4)
    sent = call(
        first_level,
        [part] * 4,
        4 * block_flops,
        [SMEM, VMEM] + [HBM] * 3,
        me,
        sibling,
        in_hbm(interface),
        *weights,
        scratch=[pltpu.VMEM((rows, features), jnp.bfloat16)]
        + [pltpu.VMEM((features, features), jnp.bfloat16)] * 2
        + [pltpu.SemaphoreType.DMA((6,))],
    )
    x = [sent[0]] + [swapped(sent[m], 2 * m) for m in (1, 2, 3)]
    weights = call(
        fetched,
        [array(2, features, features)] * 2,
        1,
        [HBM] * 2,
        *(in_hbm(w) for w in together(keep_proj, sibling_proj, sent[0])[:2]),
        scratch=[pltpu.SemaphoreType.DMA((2,))],
    )
    if few:
        x_mine, y_other, _ = together(*near, sent[0])
        (pack_near,) = call(packed, [array(2 * depth, features)], 1, [VMEM] * 2, x_mine, y_other)
        pack_far = swapped(pack_near, 1, "blk")
        d_mine, d_other = swapped(after(x_mine, x[1]), 4), swapped(after(y_other, x[1]), 2)
        x = together(*x)
    y0, y1 = call(second_level, [part] * 2, (1 << 34), [VMEM] * 4, x[0], x[1], *weights)
    done = call(third_level, [part] * 4, (1 << 34), [VMEM] * 6, x[2], x[3], y0, y1, *weights)
    back = [done[0]] + [swapped(done[m], 2 * m) for m in (1, 2, 3)]
    if not few:
        current = jnp.zeros((rows, features), jnp.bfloat16)
        for m in range(4):
            current = lax.dynamic_update_slice_in_dim(current, back[m], ((me[0] // 2 % 4) ^ m) * quarter, 0)
        return routed(current, owners, jnp.where(z[0] % 2 == 0, jnp.concatenate([mine, other]), jnp.concatenate([other, mine])))
    pieces = [mine, other, pack_near, pack_far, d_mine, d_other]
    (pack,) = call(packed, [array(8 * depth, features)], 1, [VMEM] * 6, *together(*pieces, done[0])[:6])
    matrices = [pack, swapped(pack, 1)]
    returned = [back[m] for m in (1,)]
    *returned, = call(passed, [part] * len(returned), 1 << 36, [VMEM] * len(returned), *returned)
    for m, rows_back in zip((1,), returned):
        back[m] = rows_back
    out = None
    for blocks in ((0, 1), (2, 3)):
        extra = [] if out is None else [out]
        n_block = len(blocks)
        (out,) = call(
            functools.partial(couple, blocks),
            [whole],
            8 * n_block * block_flops,
            [SMEM] * 2 + [VMEM] * (1 + n_block + len(matrices)) + [HBM] * len(extra),
            me,
            z,
            owners.reshape(-1, 128),
            *(back[m] for m in blocks),
            *matrices,
            *extra,
            scratch=[pltpu.VMEM((n_block * quarter, features), jnp.bfloat16), pltpu.SemaphoreType.DMA((2, n_block))],
            aliases={3 + n_block + len(matrices): 0} if extra else None,
        )
    return out


def solution(mesh):
    in_specs = (
        P(("leaf", "blk"), None),
        P(("leaf", "blk"), None),
        P(),
        P(),
        P("leaf", None, None),
        P("leaf", None, None),
    )
    out_specs = P(("leaf", "blk"), None)
    return jax.shard_map(local, mesh=mesh, in_specs=in_specs, out_specs=out_specs, check_vma=False)
```

```python
import functools
import jax
import jax.numpy as jnp
from jax import lax
from jax.experimental import pallas as pl
from jax.experimental.pallas import tpu as pltpu
from jax.sharding import PartitionSpec as P

BS = 64
EPSILON = 1e-06
PLACES = (0, 1), (2, 4), (5, 3), (6, 7)
VMEM = pl.BlockSpec(memory_space=pltpu.VMEM)
SMEM = pl.BlockSpec(memory_space=pltpu.SMEM)
HBM = pl.BlockSpec(memory_space=pltpu.HBM)


def swapped(value, mask, axis="leaf"):
    pairs = [(source, source ^ mask) for source in range(lax.axis_size(axis))]
    return lax.ppermute(value, axis, pairs)


def in_hbm(value):
    return pltpu.with_memory_space_constraint(value, pltpu.HBM)


def together(*values):
    return lax.optimization_barrier(values)


def after(value, *others):
    return lax.optimization_barrier((value, *others))[0]


def mixed(own, sibling, keep, cross):
    combined = jnp.dot(own, keep, preferred_element_type=jnp.float32)
    combined = combined + jnp.dot(sibling, cross, preferred_element_type=jnp.float32)
    scale_rows = lax.rsqrt(jnp.mean(combined * combined, axis=1, keepdims=True) + EPSILON)
    return (combined * scale_rows).astype(jnp.bfloat16)


def call(body, outs, flops, specs, *args, scratch=(), aliases=None):
    return pl.pallas_call(
        body,
        out_shape=[shape for shape, _ in outs],
        in_specs=specs,
        out_specs=[spec for _, spec in outs],
        scratch_shapes=list(scratch),
        input_output_aliases=aliases or {},
        cost_estimate=pl.CostEstimate(flops=flops, bytes_accessed=flops // 512, transcendentals=0),
        compiler_params=pltpu.CompilerParams(vmem_limit_bytes=24 << 20),
    )(*args)


def block_rows(me, m, size):
    return pl.ds(pl.multiple_of((((me[0] >> 1) & 3) ^ m) * size, size), size)


def first_level(me, sibling, interface, keep, cross, *rest):
    outs, (own, keep_here, cross_here, sems) = rest[:4], rest[4:]
    size = outs[0].shape[0]
    loads = [
        pltpu.make_async_copy(keep.at[0], keep_here, sems.at[4]),
        pltpu.make_async_copy(cross.at[0], cross_here, sems.at[5]),
    ]
    order = (1, 2, 3, 0)
    for m in order:
        rows = block_rows(me, m, size)
        loads.append(pltpu.make_async_copy(interface.at[rows], own.at[rows], sems.at[m]))
    for load in loads:
        load.start()
    loads[0].wait()
    loads[1].wait()
    for m, load in zip(order, loads[2:]):
        load.wait()
        rows = block_rows(me, m, size)
        outs[m][...] = mixed(own[rows, :], sibling[rows, :], keep_here[...], cross_here[...])


def second_level(x0, x1, keep, cross, out0, out1):
    out0[...] = mixed(x0[...], x1[...], keep[0], cross[0])
    out1[...] = mixed(x1[...], x0[...], keep[0], cross[0])


def third_level(x2, x3, y0, y1, keep, cross, *outs):
    y2 = mixed(x2[...], x3[...], keep[0], cross[0])
    y3 = mixed(x3[...], x2[...], keep[0], cross[0])
    outs[1][...] = mixed(y1[...], y3, keep[1], cross[1])
    outs[2][...] = mixed(y2, y0[...], keep[1], cross[1])
    outs[3][...] = mixed(y3, y1[...], keep[1], cross[1])
    outs[0][...] = mixed(y0[...], y2, keep[1], cross[1])


def masked_coupling(z, coupling, pattern, part, rest, held, shown, sems):
    loads = [pltpu.make_async_copy(pattern, shown, sems.at[0]), pltpu.make_async_copy(coupling, held, sems.at[1])]
    for load in loads:
        load.start()
    for load in loads:
        load.wait()
    for i in range(shown.shape[1]):
        row = jnp.concatenate(
            [jnp.full((BS, BS), shown[0, i, j], jnp.int32) for j in range(shown.shape[2])], axis=1
        )
        block = held[0, i * BS : (i + 1) * BS, :]
        held[0, i * BS : (i + 1) * BS, :] = jnp.where(row != 0, block, jnp.zeros_like(block))
    part[...] = held[0, half_rows(z, 0, part.shape[0]), :]
    rest[...] = held[0, half_rows(z, 1, part.shape[0]), :]


def half_rows(z, other, depth):
    return pl.ds(pl.multiple_of(((z[0] & 1) ^ other) * depth, depth), depth)


def packed(*refs):
    *parts, out = refs
    at = 0
    for part in parts:
        out[at : at + part.shape[0], :] = part[...]
        at += part.shape[0]


def couple(blocks, me, z, owners, *rest):
    n_block = len(blocks)
    xs, packs, (out, held, sems) = rest[:n_block], rest[n_block : n_block + 2], rest[-3:]
    size, features = xs[0].shape
    depth = features // 2
    lanes = owners.shape[1]
    groups = size // lanes
    diagonal = lax.broadcasted_iota(jnp.int32, (lanes, lanes), 0) == lax.broadcasted_iota(jnp.int32, (lanes, lanes), 1)
    columns_of = []
    for m in blocks:
        named = owners[pl.ds((((me[0] >> 1) & 3) ^ m) * groups, groups), :] ^ me[0]
        columns_of += [jnp.sum(jnp.where(diagonal, named[i : i + 1, :], 0), axis=1, keepdims=True) for i in range(groups)]
    relative = jnp.concatenate(columns_of, axis=0)
    parts = [half_rows(z, other, depth) for other in range(2)]
    values = [jnp.concatenate([x[:, part] for x in xs], axis=0) for part in parts]
    copies = []
    for n in range(2):
        columns = slice(n * depth, (n + 1) * depth)
        total = jnp.zeros((n_block * size, depth), jnp.float32)
        for r in range(8):
            halves = [packs[r % 2][at * depth : (at + 1) * depth, columns] for at in PLACES[r // 2]]
            each = [jnp.dot(v, half, preferred_element_type=jnp.float32) for v, half in zip(values, halves)]
            total = jnp.where(relative == r, each[0] + each[1], total)
        held[:, columns] = total.astype(jnp.bfloat16)
        for i, m in enumerate(blocks):
            to = out.at[block_rows(me, m, size), columns]
            copies.append(pltpu.make_async_copy(held.at[i * size : (i + 1) * size, columns], to, sems.at[n, i]))
            copies[-1].start()
    for copy in copies:
        copy.wait()


def passed(*refs):
    count = len(refs) // 2
    for value, out in zip(refs[:count], refs[count:]):
        out[...] = value[...]


def fetched(keep, cross, keep_here, cross_here, sems):
    loads = [
        pltpu.make_async_copy(keep.at[1:], keep_here, sems.at[0]),
        pltpu.make_async_copy(cross.at[1:], cross_here, sems.at[1]),
    ]
    for load in loads:
        load.start()
    for load in loads:
        load.wait()


def routed(current, owners, dense):
    row_count, features = current.shape
    leaves = lax.axis_size("leaf")
    capacity = 2 * row_count // leaves
    target = owners[:, 0]
    onehot = (target[:, None] == jnp.arange(leaves, dtype=jnp.int32)[None, :]).astype(jnp.int32)
    slot_index = jnp.sum(jnp.cumsum(onehot, axis=0) * onehot, axis=1) - 1
    position = target * capacity + slot_index
    outgoing = jnp.zeros((leaves * capacity, features), jnp.bfloat16).at[position].set(current)
    sectioned = outgoing.reshape(leaves, capacity, features)
    arrived = lax.all_to_all(sectioned, "leaf", split_axis=0, concat_axis=0, tiled=True)
    product = jnp.einsum("...m,mn->...n", arrived, dense, preferred_element_type=jnp.float32)
    result = product.astype(jnp.bfloat16)
    returned = lax.all_to_all(result, "leaf", split_axis=0, concat_axis=0, tiled=True)
    return returned.reshape(leaves * capacity, features)[position]


def local(interface, owners, keep_proj, sibling_proj, coupling, pattern):
    rows, features = interface.shape
    leaves = lax.axis_size("leaf")
    me = lax.axis_index("leaf").astype(jnp.int32).reshape(1)
    z = lax.axis_index("blk").astype(jnp.int32).reshape(1)
    few = leaves == 8 and lax.axis_size("blk") % 2 == 0
    quarter = rows // 4
    depth = features // 2
    block_flops = 2 * quarter * features * features

    def array(*shape, space=VMEM):
        return jax.ShapeDtypeStruct(shape, jnp.bfloat16), space

    part = array(quarter, features)
    whole = array(rows, features, space=HBM)
    matrix = array(features, features)
    weights = in_hbm(keep_proj), in_hbm(sibling_proj)

    sibling = swapped(interface, 1)
    mine, other = call(
        masked_coupling,
        [array(depth, features)] * 2,
        1,
        [SMEM] + [HBM] * 2,
        z,
        in_hbm(coupling),
        in_hbm(pattern),
        scratch=[
            pltpu.VMEM(coupling.shape, coupling.dtype),
            pltpu.VMEM(pattern.shape, pattern.dtype),
            pltpu.SemaphoreType.DMA((2,)),
        ],
    )
    if few:
        near = swapped(mine, 2), swapped(other, 4)
    sent = call(
        first_level,
        [part] * 4,
        4 * block_flops,
        [SMEM, VMEM] + [HBM] * 3,
        me,
        sibling,
        in_hbm(interface),
        *weights,
        scratch=[pltpu.VMEM((rows, features), jnp.bfloat16)]
        + [pltpu.VMEM((features, features), jnp.bfloat16)] * 2
        + [pltpu.SemaphoreType.DMA((6,))],
    )
    x = [sent[0]] + [swapped(sent[m], 2 * m) for m in (1, 2, 3)]
    weights = call(
        fetched,
        [array(2, features, features)] * 2,
        1,
        [HBM] * 2,
        *(in_hbm(w) for w in together(keep_proj, sibling_proj, sent[0])[:2]),
        scratch=[pltpu.SemaphoreType.DMA((2,))],
    )
    y0, y1 = call(second_level, [part] * 2, 1, [VMEM] * 4, x[0], x[1], *weights)
    if few:
        x_mine, y_other, _ = together(*near, sent[0])
        (pack_near,) = call(packed, [array(2 * depth, features)], 1, [VMEM] * 2, x_mine, y_other)
        pack_far = swapped(pack_near, 1, "blk")
        d_mine, d_other = swapped(after(x_mine, y0), 4), swapped(after(y_other, y0), 2)
    done = call(third_level, [part] * 4, (1 << 34), [VMEM] * 6, x[2], x[3], y0, y1, *weights)
    back = [done[0]] + [swapped(done[m], 2 * m) for m in (1, 2, 3)]
    if not few:
        current = jnp.zeros((rows, features), jnp.bfloat16)
        for m in range(4):
            current = lax.dynamic_update_slice_in_dim(current, back[m], ((me[0] // 2 % 4) ^ m) * quarter, 0)
        return routed(current, owners, jnp.where(z[0] % 2 == 0, jnp.concatenate([mine, other]), jnp.concatenate([other, mine])))
    pieces = [mine, other, pack_near, pack_far, d_mine, d_other]
    (pack,) = call(packed, [array(8 * depth, features)], 1, [VMEM] * 6, *together(*pieces, done[0])[:6])
    matrices = [pack, swapped(pack, 1)]
    returned = [back[m] for m in (1,)]
    *returned, = call(passed, [part] * len(returned), 1 << 36, [VMEM] * len(returned), *returned)
    for m, rows_back in zip((1,), returned):
        back[m] = rows_back
    out = None
    for blocks in ((0, 1), (2, 3)):
        extra = [] if out is None else [out]
        n_block = len(blocks)
        (out,) = call(
            functools.partial(couple, blocks),
            [whole],
            8 * n_block * block_flops,
            [SMEM] * 2 + [VMEM] * (1 + n_block + len(matrices)) + [HBM] * len(extra),
            me,
            z,
            owners.reshape(-1, 128),
            *(back[m] for m in blocks),
            *matrices,
            *extra,
            scratch=[pltpu.VMEM((n_block * quarter, features), jnp.bfloat16), pltpu.SemaphoreType.DMA((2, n_block))],
            aliases={3 + n_block + len(matrices): 0} if extra else None,
        )
    return out


def solution(mesh):
    in_specs = (
        P(("leaf", "blk"), None),
        P(("leaf", "blk"), None),
        P(),
        P(),
        P("leaf", None, None),
        P("leaf", None, None),
    )
    out_specs = P(("leaf", "blk"), None)
    return jax.shard_map(local, mesh=mesh, in_specs=in_specs, out_specs=out_specs, check_vma=False)
```

```python
import functools
import jax
import jax.numpy as jnp
from jax import lax
from jax.experimental import pallas as pl
from jax.experimental.pallas import tpu as pltpu
from jax.sharding import PartitionSpec as P

BS = 64
EPSILON = 1e-06
PLACES = (0, 1), (2, 4), (5, 3), (6, 7)
VMEM = pl.BlockSpec(memory_space=pltpu.VMEM)
SMEM = pl.BlockSpec(memory_space=pltpu.SMEM)
HBM = pl.BlockSpec(memory_space=pltpu.HBM)


def swapped(value, mask, axis="leaf"):
    pairs = [(source, source ^ mask) for source in range(lax.axis_size(axis))]
    return lax.ppermute(value, axis, pairs)


def in_hbm(value):
    return pltpu.with_memory_space_constraint(value, pltpu.HBM)


def together(*values):
    return lax.optimization_barrier(values)


def after(value, *others):
    return lax.optimization_barrier((value, *others))[0]


def mixed(own, sibling, keep, cross):
    combined = jnp.dot(own, keep, preferred_element_type=jnp.float32)
    combined = combined + jnp.dot(sibling, cross, preferred_element_type=jnp.float32)
    scale_rows = lax.rsqrt(jnp.mean(combined * combined, axis=1, keepdims=True) + EPSILON)
    return (combined * scale_rows).astype(jnp.bfloat16)


def call(body, outs, flops, specs, *args, scratch=(), aliases=None):
    return pl.pallas_call(
        body,
        out_shape=[shape for shape, _ in outs],
        in_specs=specs,
        out_specs=[spec for _, spec in outs],
        scratch_shapes=list(scratch),
        input_output_aliases=aliases or {},
        cost_estimate=pl.CostEstimate(flops=flops, bytes_accessed=flops // 512, transcendentals=0),
        compiler_params=pltpu.CompilerParams(vmem_limit_bytes=24 << 20),
    )(*args)


def block_rows(me, m, size):
    return pl.ds(pl.multiple_of((((me[0] >> 1) & 3) ^ m) * size, size), size)


def first_level(me, sibling, interface, keep, cross, *rest):
    outs, (own, keep_here, cross_here, sems) = rest[:4], rest[4:]
    size = outs[0].shape[0]
    loads = [
        pltpu.make_async_copy(keep.at[0], keep_here, sems.at[4]),
        pltpu.make_async_copy(cross.at[0], cross_here, sems.at[5]),
    ]
    order = (1, 2, 3, 0)
    for m in order:
        rows = block_rows(me, m, size)
        loads.append(pltpu.make_async_copy(interface.at[rows], own.at[rows], sems.at[m]))
    for load in loads:
        load.start()
    loads[0].wait()
    loads[1].wait()
    for m, load in zip(order, loads[2:]):
        load.wait()
        rows = block_rows(me, m, size)
        outs[m][...] = mixed(own[rows, :], sibling[rows, :], keep_here[...], cross_here[...])


def second_level(x0, x1, keep, cross, out0, out1):
    out0[...] = mixed(x0[...], x1[...], keep[0], cross[0])
    out1[...] = mixed(x1[...], x0[...], keep[0], cross[0])


def third_level(x2, x3, y0, y1, keep, cross, *outs):
    y2 = mixed(x2[...], x3[...], keep[0], cross[0])
    y3 = mixed(x3[...], x2[...], keep[0], cross[0])
    outs[1][...] = mixed(y1[...], y3, keep[1], cross[1])
    outs[2][...] = mixed(y2, y0[...], keep[1], cross[1])
    outs[3][...] = mixed(y3, y1[...], keep[1], cross[1])
    outs[0][...] = mixed(y0[...], y2, keep[1], cross[1])


def masked_coupling(z, coupling, pattern, part, rest, held, shown, sems):
    loads = [pltpu.make_async_copy(pattern, shown, sems.at[0]), pltpu.make_async_copy(coupling, held, sems.at[1])]
    for load in loads:
        load.start()
    for load in loads:
        load.wait()
    for i in range(shown.shape[1]):
        row = jnp.concatenate(
            [jnp.full((BS, BS), shown[0, i, j], jnp.int32) for j in range(shown.shape[2])], axis=1
        )
        block = held[0, i * BS : (i + 1) * BS, :]
        held[0, i * BS : (i + 1) * BS, :] = jnp.where(row != 0, block, jnp.zeros_like(block))
    part[...] = held[0, half_rows(z, 0, part.shape[0]), :]
    rest[...] = held[0, half_rows(z, 1, part.shape[0]), :]


def half_rows(z, other, depth):
    return pl.ds(pl.multiple_of(((z[0] & 1) ^ other) * depth, depth), depth)


def packed(*refs):
    *parts, out = refs
    at = 0
    for part in parts:
        out[at : at + part.shape[0], :] = part[...]
        at += part.shape[0]


def couple(blocks, me, z, owners, *rest):
    n_block = len(blocks)
    xs, packs, (out, held, sems) = rest[:n_block], rest[n_block : n_block + 2], rest[-3:]
    size, features = xs[0].shape
    depth = features // 2
    lanes = owners.shape[1]
    groups = size // lanes
    diagonal = lax.broadcasted_iota(jnp.int32, (lanes, lanes), 0) == lax.broadcasted_iota(jnp.int32, (lanes, lanes), 1)
    columns_of = []
    for m in blocks:
        named = owners[pl.ds((((me[0] >> 1) & 3) ^ m) * groups, groups), :] ^ me[0]
        columns_of += [jnp.sum(jnp.where(diagonal, named[i : i + 1, :], 0), axis=1, keepdims=True) for i in range(groups)]
    relative = jnp.concatenate(columns_of, axis=0)
    parts = [half_rows(z, other, depth) for other in range(2)]
    values = [jnp.concatenate([x[:, part] for x in xs], axis=0) for part in parts]
    copies = []
    for n in range(2):
        columns = slice(n * depth, (n + 1) * depth)
        total = jnp.zeros((n_block * size, depth), jnp.float32)
        for r in range(8):
            halves = [packs[r % 2][at * depth : (at + 1) * depth, columns] for at in PLACES[r // 2]]
            each = [jnp.dot(v, half, preferred_element_type=jnp.float32) for v, half in zip(values, halves)]
            total = jnp.where(relative == r, each[0] + each[1], total)
        held[:, columns] = total.astype(jnp.bfloat16)
        for i, m in enumerate(blocks):
            to = out.at[block_rows(me, m, size), columns]
            copies.append(pltpu.make_async_copy(held.at[i * size : (i + 1) * size, columns], to, sems.at[n, i]))
            copies[-1].start()
    for copy in copies:
        copy.wait()


def passed(*refs):
    count = len(refs) // 2
    for value, out in zip(refs[:count], refs[count:]):
        out[...] = value[...]


def fetched(keep, cross, keep_here, cross_here, sems):
    loads = [
        pltpu.make_async_copy(keep.at[1:], keep_here, sems.at[0]),
        pltpu.make_async_copy(cross.at[1:], cross_here, sems.at[1]),
    ]
    for load in loads:
        load.start()
    for load in loads:
        load.wait()


def routed(current, owners, dense):
    row_count, features = current.shape
    leaves = lax.axis_size("leaf")
    capacity = 2 * row_count // leaves
    target = owners[:, 0]
    onehot = (target[:, None] == jnp.arange(leaves, dtype=jnp.int32)[None, :]).astype(jnp.int32)
    slot_index = jnp.sum(jnp.cumsum(onehot, axis=0) * onehot, axis=1) - 1
    position = target * capacity + slot_index
    outgoing = jnp.zeros((leaves * capacity, features), jnp.bfloat16).at[position].set(current)
    sectioned = outgoing.reshape(leaves, capacity, features)
    arrived = lax.all_to_all(sectioned, "leaf", split_axis=0, concat_axis=0, tiled=True)
    product = jnp.einsum("...m,mn->...n", arrived, dense, preferred_element_type=jnp.float32)
    result = product.astype(jnp.bfloat16)
    returned = lax.all_to_all(result, "leaf", split_axis=0, concat_axis=0, tiled=True)
    return returned.reshape(leaves * capacity, features)[position]


def local(interface, owners, keep_proj, sibling_proj, coupling, pattern):
    rows, features = interface.shape
    leaves = lax.axis_size("leaf")
    me = lax.axis_index("leaf").astype(jnp.int32).reshape(1)
    z = lax.axis_index("blk").astype(jnp.int32).reshape(1)
    few = leaves == 8 and lax.axis_size("blk") % 2 == 0
    quarter = rows // 4
    depth = features // 2
    block_flops = 2 * quarter * features * features

    def array(*shape, space=VMEM):
        return jax.ShapeDtypeStruct(shape, jnp.bfloat16), space

    part = array(quarter, features)
    whole = array(rows, features, space=HBM)
    matrix = array(features, features)
    weights = in_hbm(keep_proj), in_hbm(sibling_proj)

    sibling = swapped(interface, 1)
    mine, other = call(
        masked_coupling,
        [array(depth, features)] * 2,
        1,
        [SMEM] + [HBM] * 2,
        z,
        in_hbm(coupling),
        in_hbm(pattern),
        scratch=[
            pltpu.VMEM(coupling.shape, coupling.dtype),
            pltpu.SMEM(pattern.shape, pattern.dtype),
            pltpu.SemaphoreType.DMA((2,)),
        ],
    )
    if few:
        near = swapped(mine, 2), swapped(other, 4)
    sent = call(
        first_level,
        [part] * 4,
        4 * block_flops,
        [SMEM, VMEM] + [HBM] * 3,
        me,
        sibling,
        in_hbm(interface),
        *weights,
        scratch=[pltpu.VMEM((rows, features), jnp.bfloat16)]
        + [pltpu.VMEM((features, features), jnp.bfloat16)] * 2
        + [pltpu.SemaphoreType.DMA((6,))],
    )
    x = [sent[0]] + [swapped(sent[m], 2 * m) for m in (1, 2, 3)]
    weights = call(
        fetched,
        [array(2, features, features)] * 2,
        1,
        [HBM] * 2,
        *(in_hbm(w) for w in together(keep_proj, sibling_proj, sent[0])[:2]),
        scratch=[pltpu.SemaphoreType.DMA((2,))],
    )
    y0, y1 = call(second_level, [part] * 2, 1, [VMEM] * 4, x[0], x[1], *weights)
    if few:
        x_mine, y_other, _ = together(*near, sent[0])
        (pack_near,) = call(packed, [array(2 * depth, features)], 1, [VMEM] * 2, x_mine, y_other)
        pack_far = swapped(pack_near, 1, "blk")
        d_mine, d_other = swapped(after(x_mine, y0), 4), swapped(after(y_other, y0), 2)
    done = call(third_level, [part] * 4, (1 << 34), [VMEM] * 6, x[2], x[3], y0, y1, *weights)
    back = [done[0]] + [swapped(done[m], 2 * m) for m in (1, 2, 3)]
    if not few:
        current = jnp.zeros((rows, features), jnp.bfloat16)
        for m in range(4):
            current = lax.dynamic_update_slice_in_dim(current, back[m], ((me[0] // 2 % 4) ^ m) * quarter, 0)
        return routed(current, owners, jnp.where(z[0] % 2 == 0, jnp.concatenate([mine, other]), jnp.concatenate([other, mine])))
    pieces = [mine, other, pack_near, pack_far, d_mine, d_other]
    (pack,) = call(packed, [array(8 * depth, features)], 1, [VMEM] * 6, *together(*pieces, done[0])[:6])
    matrices = [pack, swapped(pack, 1)]
    returned = [back[m] for m in (1,)]
    *returned, = call(passed, [part] * len(returned), 1 << 36, [VMEM] * len(returned), *returned)
    for m, rows_back in zip((1,), returned):
        back[m] = rows_back
    out = None
    for blocks in ((0, 1), (2, 3)):
        extra = [] if out is None else [out]
        n_block = len(blocks)
        (out,) = call(
            functools.partial(couple, blocks),
            [whole],
            8 * n_block * block_flops,
            [SMEM] * 2 + [VMEM] * (1 + n_block + len(matrices)) + [HBM] * len(extra),
            me,
            z,
            owners.reshape(-1, 128),
            *(back[m] for m in blocks),
            *matrices,
            *extra,
            scratch=[pltpu.VMEM((n_block * quarter, features), jnp.bfloat16), pltpu.SemaphoreType.DMA((2, n_block))],
            aliases={3 + n_block + len(matrices): 0} if extra else None,
        )
    return out


def solution(mesh):
    in_specs = (
        P(("leaf", "blk"), None),
        P(("leaf", "blk"), None),
        P(),
        P(),
        P("leaf", None, None),
        P("leaf", None, None),
    )
    out_specs = P(("leaf", "blk"), None)
    return jax.shard_map(local, mesh=mesh, in_specs=in_specs, out_specs=out_specs, check_vma=False)
```

```python
import functools
import jax
import jax.numpy as jnp
from jax import lax
from jax.experimental import pallas as pl
from jax.experimental.pallas import tpu as pltpu
from jax.sharding import PartitionSpec as P

BS = 64
EPSILON = 1e-06
PLACES = (0, 1), (2, 4), (5, 3), (6, 7)
VMEM = pl.BlockSpec(memory_space=pltpu.VMEM)
SMEM = pl.BlockSpec(memory_space=pltpu.SMEM)
HBM = pl.BlockSpec(memory_space=pltpu.HBM)


def swapped(value, mask, axis="leaf"):
    pairs = [(source, source ^ mask) for source in range(lax.axis_size(axis))]
    return lax.ppermute(value, axis, pairs)


def in_hbm(value):
    return pltpu.with_memory_space_constraint(value, pltpu.HBM)


def together(*values):
    return lax.optimization_barrier(values)


def after(value, *others):
    return lax.optimization_barrier((value, *others))[0]


def mixed(own, sibling, keep, cross):
    combined = jnp.dot(own, keep, preferred_element_type=jnp.float32)
    return normal(combined + jnp.dot(sibling, cross, preferred_element_type=jnp.float32))


def normal(combined):
    scale_rows = lax.rsqrt(jnp.mean(combined * combined, axis=1, keepdims=True) + EPSILON)
    return (combined * scale_rows).astype(jnp.bfloat16)


def call(body, outs, flops, specs, *args, scratch=(), aliases=None):
    return pl.pallas_call(
        body,
        out_shape=[shape for shape, _ in outs],
        in_specs=specs,
        out_specs=[spec for _, spec in outs],
        scratch_shapes=list(scratch),
        input_output_aliases=aliases or {},
        cost_estimate=pl.CostEstimate(flops=flops, bytes_accessed=flops // 512, transcendentals=0),
        compiler_params=pltpu.CompilerParams(vmem_limit_bytes=24 << 20),
    )(*args)


def block_rows(me, m, size):
    return pl.ds(pl.multiple_of((((me[0] >> 1) & 3) ^ m) * size, size), size)


def first_level(me, sibling, interface, keep, cross, *rest):
    outs, (own, keep_here, cross_here, sems) = rest[:4], rest[4:]
    size = outs[0].shape[0]
    order = (1, 2, 3, 0)
    loads = [
        pltpu.make_async_copy(cross.at[0], cross_here, sems.at[5]),
        pltpu.make_async_copy(keep.at[0], keep_here, sems.at[4]),
    ]
    for m in order:
        rows = block_rows(me, m, size)
        loads.append(pltpu.make_async_copy(interface.at[rows], own.at[rows], sems.at[m]))
    for load in loads:
        load.start()
    loads[0].wait()
    terms = []
    for m in order:
        terms.append(jnp.dot(sibling[block_rows(me, m, size), :], cross_here[...], preferred_element_type=jnp.float32))
    loads[1].wait()
    for m, load, term in zip(order, loads[2:], terms):
        load.wait()
        rows = block_rows(me, m, size)
        outs[m][...] = normal(jnp.dot(own[rows, :], keep_here[...], preferred_element_type=jnp.float32) + term)


def second_level(x0, x1, keep, cross, out0, out1):
    out0[...] = mixed(x0[...], x1[...], keep[0], cross[0])
    out1[...] = mixed(x1[...], x0[...], keep[0], cross[0])


def third_level(x2, x3, y0, y1, keep, cross, *outs):
    y2 = mixed(x2[...], x3[...], keep[0], cross[0])
    y3 = mixed(x3[...], x2[...], keep[0], cross[0])
    outs[1][...] = mixed(y1[...], y3, keep[1], cross[1])
    outs[2][...] = mixed(y2, y0[...], keep[1], cross[1])
    outs[3][...] = mixed(y3, y1[...], keep[1], cross[1])
    outs[0][...] = mixed(y0[...], y2, keep[1], cross[1])


def masked_coupling(z, coupling, pattern, part, rest, held, shown, sems):
    loads = [pltpu.make_async_copy(pattern, shown, sems.at[0]), pltpu.make_async_copy(coupling, held, sems.at[1])]
    for load in loads:
        load.start()
    for load in loads:
        load.wait()
    for i in range(shown.shape[1]):
        row = jnp.concatenate(
            [jnp.full((BS, BS), shown[0, i, j], jnp.int32) for j in range(shown.shape[2])], axis=1
        )
        block = held[0, i * BS : (i + 1) * BS, :]
        held[0, i * BS : (i + 1) * BS, :] = jnp.where(row != 0, block, jnp.zeros_like(block))
    part[...] = held[0, half_rows(z, 0, part.shape[0]), :]
    rest[...] = held[0, half_rows(z, 1, part.shape[0]), :]


def half_rows(z, other, depth):
    return pl.ds(pl.multiple_of(((z[0] & 1) ^ other) * depth, depth), depth)


def packed(*refs):
    *parts, out = refs
    at = 0
    for part in parts:
        out[at : at + part.shape[0], :] = part[...]
        at += part.shape[0]


def couple(blocks, me, z, owners, *rest):
    n_block = len(blocks)
    xs, packs, (out, held, sems) = rest[:n_block], rest[n_block : n_block + 2], rest[-3:]
    size, features = xs[0].shape
    depth = features // 2
    lanes = owners.shape[1]
    groups = size // lanes
    diagonal = lax.broadcasted_iota(jnp.int32, (lanes, lanes), 0) == lax.broadcasted_iota(jnp.int32, (lanes, lanes), 1)
    columns_of = []
    for m in blocks:
        named = owners[pl.ds((((me[0] >> 1) & 3) ^ m) * groups, groups), :] ^ me[0]
        columns_of += [jnp.sum(jnp.where(diagonal, named[i : i + 1, :], 0), axis=1, keepdims=True) for i in range(groups)]
    relative = jnp.concatenate(columns_of, axis=0)
    parts = [half_rows(z, other, depth) for other in range(2)]
    values = [jnp.concatenate([x[:, part] for x in xs], axis=0) for part in parts]
    copies = []
    for n in range(2):
        columns = slice(n * depth, (n + 1) * depth)
        total = jnp.zeros((n_block * size, depth), jnp.float32)
        for r in range(8):
            halves = [packs[r % 2][at * depth : (at + 1) * depth, columns] for at in PLACES[r // 2]]
            each = [jnp.dot(v, half, preferred_element_type=jnp.float32) for v, half in zip(values, halves)]
            total = jnp.where(relative == r, each[0] + each[1], total)
        held[:, columns] = total.astype(jnp.bfloat16)
        for i, m in enumerate(blocks):
            to = out.at[block_rows(me, m, size), columns]
            copies.append(pltpu.make_async_copy(held.at[i * size : (i + 1) * size, columns], to, sems.at[n, i]))
            copies[-1].start()
    for copy in copies:
        copy.wait()


def passed(*refs):
    count = len(refs) // 2
    for value, out in zip(refs[:count], refs[count:]):
        out[...] = value[...]


def fetched(keep, cross, keep_here, cross_here, sems):
    loads = [
        pltpu.make_async_copy(keep.at[1:], keep_here, sems.at[0]),
        pltpu.make_async_copy(cross.at[1:], cross_here, sems.at[1]),
    ]
    for load in loads:
        load.start()
    for load in loads:
        load.wait()


def routed(current, owners, dense):
    row_count, features = current.shape
    leaves = lax.axis_size("leaf")
    capacity = 2 * row_count // leaves
    target = owners[:, 0]
    onehot = (target[:, None] == jnp.arange(leaves, dtype=jnp.int32)[None, :]).astype(jnp.int32)
    slot_index = jnp.sum(jnp.cumsum(onehot, axis=0) * onehot, axis=1) - 1
    position = target * capacity + slot_index
    outgoing = jnp.zeros((leaves * capacity, features), jnp.bfloat16).at[position].set(current)
    sectioned = outgoing.reshape(leaves, capacity, features)
    arrived = lax.all_to_all(sectioned, "leaf", split_axis=0, concat_axis=0, tiled=True)
    product = jnp.einsum("...m,mn->...n", arrived, dense, preferred_element_type=jnp.float32)
    result = product.astype(jnp.bfloat16)
    returned = lax.all_to_all(result, "leaf", split_axis=0, concat_axis=0, tiled=True)
    return returned.reshape(leaves * capacity, features)[position]


def local(interface, owners, keep_proj, sibling_proj, coupling, pattern):
    rows, features = interface.shape
    leaves = lax.axis_size("leaf")
    me = lax.axis_index("leaf").astype(jnp.int32).reshape(1)
    z = lax.axis_index("blk").astype(jnp.int32).reshape(1)
    few = leaves == 8 and lax.axis_size("blk") % 2 == 0
    quarter = rows // 4
    depth = features // 2
    block_flops = 2 * quarter * features * features

    def array(*shape, space=VMEM):
        return jax.ShapeDtypeStruct(shape, jnp.bfloat16), space

    part = array(quarter, features)
    whole = array(rows, features, space=HBM)
    matrix = array(features, features)
    weights = in_hbm(keep_proj), in_hbm(sibling_proj)

    sibling = swapped(interface, 1)
    mine, other = call(
        masked_coupling,
        [array(depth, features)] * 2,
        1,
        [SMEM] + [HBM] * 2,
        z,
        in_hbm(coupling),
        in_hbm(pattern),
        scratch=[
            pltpu.VMEM(coupling.shape, coupling.dtype),
            pltpu.SMEM(pattern.shape, pattern.dtype),
            pltpu.SemaphoreType.DMA((2,)),
        ],
    )
    if few:
        near = swapped(mine, 2), swapped(other, 4)
    sent = call(
        first_level,
        [part] * 4,
        4 * block_flops,
        [SMEM, VMEM] + [HBM] * 3,
        me,
        sibling,
        in_hbm(interface),
        *weights,
        scratch=[pltpu.VMEM((rows, features), jnp.bfloat16)]
        + [pltpu.VMEM((features, features), jnp.bfloat16)] * 2
        + [pltpu.SemaphoreType.DMA((6,))],
    )
    x = [sent[0]] + [swapped(sent[m], 2 * m) for m in (1, 2, 3)]
    weights = call(
        fetched,
        [array(2, features, features)] * 2,
        1,
        [HBM] * 2,
        *(in_hbm(w) for w in together(keep_proj, sibling_proj, sent[0])[:2]),
        scratch=[pltpu.SemaphoreType.DMA((2,))],
    )
    y0, y1 = call(second_level, [part] * 2, 1, [VMEM] * 4, x[0], x[1], *weights)
    if few:
        x_mine, y_other, _ = together(*near, sent[0])
        (pack_near,) = call(packed, [array(2 * depth, features)], 1, [VMEM] * 2, x_mine, y_other)
        pack_far = swapped(pack_near, 1, "blk")
        d_mine, d_other = swapped(after(x_mine, y0), 4), swapped(after(y_other, y0), 2)
    done = call(third_level, [part] * 4, (1 << 34), [VMEM] * 6, x[2], x[3], y0, y1, *weights)
    back = [done[0]] + [swapped(done[m], 2 * m) for m in (1, 2, 3)]
    if not few:
        current = jnp.zeros((rows, features), jnp.bfloat16)
        for m in range(4):
            current = lax.dynamic_update_slice_in_dim(current, back[m], ((me[0] // 2 % 4) ^ m) * quarter, 0)
        return routed(current, owners, jnp.where(z[0] % 2 == 0, jnp.concatenate([mine, other]), jnp.concatenate([other, mine])))
    pieces = [mine, other, pack_near, pack_far, d_mine, d_other]
    (pack,) = call(packed, [array(8 * depth, features)], 1, [VMEM] * 6, *together(*pieces, done[0])[:6])
    matrices = [pack, swapped(pack, 1)]
    returned = [back[m] for m in (1,)]
    *returned, = call(passed, [part] * len(returned), 1 << 36, [VMEM] * len(returned), *returned)
    for m, rows_back in zip((1,), returned):
        back[m] = rows_back
    out = None
    for blocks in ((0, 1), (2, 3)):
        extra = [] if out is None else [out]
        n_block = len(blocks)
        (out,) = call(
            functools.partial(couple, blocks),
            [whole],
            8 * n_block * block_flops,
            [SMEM] * 2 + [VMEM] * (1 + n_block + len(matrices)) + [HBM] * len(extra),
            me,
            z,
            owners.reshape(-1, 128),
            *(back[m] for m in blocks),
            *matrices,
            *extra,
            scratch=[pltpu.VMEM((n_block * quarter, features), jnp.bfloat16), pltpu.SemaphoreType.DMA((2, n_block))],
            aliases={3 + n_block + len(matrices): 0} if extra else None,
        )
    return out


def solution(mesh):
    in_specs = (
        P(("leaf", "blk"), None),
        P(("leaf", "blk"), None),
        P(),
        P(),
        P("leaf", None, None),
        P("leaf", None, None),
    )
    out_specs = P(("leaf", "blk"), None)
    return jax.shard_map(local, mesh=mesh, in_specs=in_specs, out_specs=out_specs, check_vma=False)
```

```python
import functools
import jax
import jax.numpy as jnp
from jax import lax
from jax.experimental import pallas as pl
from jax.experimental.pallas import tpu as pltpu
from jax.sharding import PartitionSpec as P

BS = 64
EPSILON = 1e-06
PLACES = (0, 1), (2, 4), (5, 3), (6, 7)
VMEM = pl.BlockSpec(memory_space=pltpu.VMEM)
SMEM = pl.BlockSpec(memory_space=pltpu.SMEM)
HBM = pl.BlockSpec(memory_space=pltpu.HBM)


def swapped(value, mask, axis="leaf"):
    pairs = [(source, source ^ mask) for source in range(lax.axis_size(axis))]
    return lax.ppermute(value, axis, pairs)


def in_hbm(value):
    return pltpu.with_memory_space_constraint(value, pltpu.HBM)


def together(*values):
    return lax.optimization_barrier(values)


def after(value, *others):
    return lax.optimization_barrier((value, *others))[0]


def mixed(own, sibling, keep, cross):
    combined = jnp.dot(own, keep, preferred_element_type=jnp.float32)
    return normal(combined + jnp.dot(sibling, cross, preferred_element_type=jnp.float32))


def normal(combined):
    scale_rows = lax.rsqrt(jnp.mean(combined * combined, axis=1, keepdims=True) + EPSILON)
    return (combined * scale_rows).astype(jnp.bfloat16)


def call(body, outs, flops, specs, *args, scratch=(), aliases=None):
    return pl.pallas_call(
        body,
        out_shape=[shape for shape, _ in outs],
        in_specs=specs,
        out_specs=[spec for _, spec in outs],
        scratch_shapes=list(scratch),
        input_output_aliases=aliases or {},
        cost_estimate=pl.CostEstimate(flops=flops, bytes_accessed=flops // 512, transcendentals=0),
        compiler_params=pltpu.CompilerParams(vmem_limit_bytes=24 << 20),
    )(*args)


def block_rows(me, m, size):
    return pl.ds(pl.multiple_of((((me[0] >> 1) & 3) ^ m) * size, size), size)


def first_level(me, sibling, interface, keep, cross, *rest):
    outs, (own, keep_here, cross_here, sems) = rest[:4], rest[4:]
    size = outs[0].shape[0]
    order = (1, 2, 3, 0)
    loads = [
        pltpu.make_async_copy(cross.at[0], cross_here, sems.at[5]),
        pltpu.make_async_copy(keep.at[0], keep_here, sems.at[4]),
    ]
    for m in order:
        rows = block_rows(me, m, size)
        loads.append(pltpu.make_async_copy(interface.at[rows], own.at[rows], sems.at[m]))
    for load in loads:
        load.start()
    loads[0].wait()
    terms = []
    for m in order:
        terms.append(jnp.dot(sibling[block_rows(me, m, size), :], cross_here[...], preferred_element_type=jnp.float32))
    loads[1].wait()
    for m, load, term in zip(order, loads[2:], terms):
        load.wait()
        rows = block_rows(me, m, size)
        outs[m][...] = normal(jnp.dot(own[rows, :], keep_here[...], preferred_element_type=jnp.float32) + term)


def second_level(x0, x1, keep, cross, out0, out1):
    out0[...] = mixed(x0[...], x1[...], keep[0], cross[0])
    out1[...] = mixed(x1[...], x0[...], keep[0], cross[0])


def third_level(x2, x3, y0, y1, keep, cross, *outs):
    y2 = mixed(x2[...], x3[...], keep[0], cross[0])
    y3 = mixed(x3[...], x2[...], keep[0], cross[0])
    outs[1][...] = mixed(y1[...], y3, keep[1], cross[1])
    outs[2][...] = mixed(y2, y0[...], keep[1], cross[1])
    outs[3][...] = mixed(y3, y1[...], keep[1], cross[1])
    outs[0][...] = mixed(y0[...], y2, keep[1], cross[1])


def masked_coupling(z, coupling, pattern, part, rest, held, shown, sems):
    loads = [pltpu.make_async_copy(pattern, shown, sems.at[0]), pltpu.make_async_copy(coupling, held, sems.at[1])]
    for load in loads:
        load.start()
    for load in loads:
        load.wait()
    for i in range(shown.shape[1]):
        row = jnp.concatenate(
            [jnp.full((BS, BS), shown[0, i, j], jnp.int32) for j in range(shown.shape[2])], axis=1
        )
        block = held[0, i * BS : (i + 1) * BS, :]
        held[0, i * BS : (i + 1) * BS, :] = jnp.where(row != 0, block, jnp.zeros_like(block))
    part[...] = held[0, half_rows(z, 0, part.shape[0]), :]
    rest[...] = held[0, half_rows(z, 1, part.shape[0]), :]


def half_rows(z, other, depth):
    return pl.ds(pl.multiple_of(((z[0] & 1) ^ other) * depth, depth), depth)


def packed(*refs):
    *parts, out = refs
    at = 0
    for part in parts:
        out[at : at + part.shape[0], :] = part[...]
        at += part.shape[0]


def named(me, owners, out):
    lanes = owners.shape[1]
    groups = owners.shape[0] // 4
    diagonal = lax.broadcasted_iota(jnp.int32, (lanes, lanes), 0) == lax.broadcasted_iota(jnp.int32, (lanes, lanes), 1)
    for m in range(4):
        block = owners[pl.ds((((me[0] >> 1) & 3) ^ m) * groups, groups), :] ^ me[0]
        for i in range(groups):
            column = jnp.sum(jnp.where(diagonal, block[i : i + 1, :], 0), axis=1, keepdims=True)
            at = (m * groups + i) * lanes
            out[at : at + lanes, :] = jnp.broadcast_to(column, (lanes, lanes))


def couple(blocks, me, z, owners, *rest):
    n_block = len(blocks)
    xs, packs, (out, held, sems) = rest[:n_block], rest[n_block : n_block + 2], rest[-3:]
    size, features = xs[0].shape
    depth = features // 2
    wide = jnp.concatenate([owners[m * size : (m + 1) * size, :] for m in blocks], axis=0)
    relative = jnp.concatenate([wide] * (depth // wide.shape[1]), axis=1)
    parts = [half_rows(z, other, depth) for other in range(2)]
    values = [jnp.concatenate([x[:, part] for x in xs], axis=0) for part in parts]
    copies = []
    for n in range(2):
        columns = slice(n * depth, (n + 1) * depth)
        total = jnp.zeros((n_block * size, depth), jnp.float32)
        for r in range(8):
            halves = [packs[r % 2][at * depth : (at + 1) * depth, columns] for at in PLACES[r // 2]]
            each = [jnp.dot(v, half, preferred_element_type=jnp.float32) for v, half in zip(values, halves)]
            total = jnp.where(relative == r, each[0] + each[1], total)
        held[:, columns] = total.astype(jnp.bfloat16)
        for i, m in enumerate(blocks):
            to = out.at[block_rows(me, m, size), columns]
            copies.append(pltpu.make_async_copy(held.at[i * size : (i + 1) * size, columns], to, sems.at[n, i]))
            copies[-1].start()
    for copy in copies:
        copy.wait()


def passed(*refs):
    count = len(refs) // 2
    for value, out in zip(refs[:count], refs[count:]):
        out[...] = value[...]


def fetched(keep, cross, keep_here, cross_here, sems):
    loads = [
        pltpu.make_async_copy(keep.at[1:], keep_here, sems.at[0]),
        pltpu.make_async_copy(cross.at[1:], cross_here, sems.at[1]),
    ]
    for load in loads:
        load.start()
    for load in loads:
        load.wait()


def routed(current, owners, dense):
    row_count, features = current.shape
    leaves = lax.axis_size("leaf")
    capacity = 2 * row_count // leaves
    target = owners[:, 0]
    onehot = (target[:, None] == jnp.arange(leaves, dtype=jnp.int32)[None, :]).astype(jnp.int32)
    slot_index = jnp.sum(jnp.cumsum(onehot, axis=0) * onehot, axis=1) - 1
    position = target * capacity + slot_index
    outgoing = jnp.zeros((leaves * capacity, features), jnp.bfloat16).at[position].set(current)
    sectioned = outgoing.reshape(leaves, capacity, features)
    arrived = lax.all_to_all(sectioned, "leaf", split_axis=0, concat_axis=0, tiled=True)
    product = jnp.einsum("...m,mn->...n", arrived, dense, preferred_element_type=jnp.float32)
    result = product.astype(jnp.bfloat16)
    returned = lax.all_to_all(result, "leaf", split_axis=0, concat_axis=0, tiled=True)
    return returned.reshape(leaves * capacity, features)[position]


def local(interface, owners, keep_proj, sibling_proj, coupling, pattern):
    rows, features = interface.shape
    leaves = lax.axis_size("leaf")
    me = lax.axis_index("leaf").astype(jnp.int32).reshape(1)
    z = lax.axis_index("blk").astype(jnp.int32).reshape(1)
    few = leaves == 8 and lax.axis_size("blk") % 2 == 0
    quarter = rows // 4
    depth = features // 2
    block_flops = 2 * quarter * features * features

    def array(*shape, space=VMEM):
        return jax.ShapeDtypeStruct(shape, jnp.bfloat16), space

    part = array(quarter, features)
    whole = array(rows, features, space=HBM)
    matrix = array(features, features)
    weights = in_hbm(keep_proj), in_hbm(sibling_proj)

    sibling = swapped(interface, 1)
    mine, other = call(
        masked_coupling,
        [array(depth, features)] * 2,
        1,
        [SMEM] + [HBM] * 2,
        z,
        in_hbm(coupling),
        in_hbm(pattern),
        scratch=[
            pltpu.VMEM(coupling.shape, coupling.dtype),
            pltpu.SMEM(pattern.shape, pattern.dtype),
            pltpu.SemaphoreType.DMA((2,)),
        ],
    )
    if few:
        near = swapped(mine, 2), swapped(other, 4)
    sent = call(
        first_level,
        [part] * 4,
        4 * block_flops,
        [SMEM, VMEM] + [HBM] * 3,
        me,
        sibling,
        in_hbm(interface),
        *weights,
        scratch=[pltpu.VMEM((rows, features), jnp.bfloat16)]
        + [pltpu.VMEM((features, features), jnp.bfloat16)] * 2
        + [pltpu.SemaphoreType.DMA((6,))],
    )
    x = [sent[0]] + [swapped(sent[m], 2 * m) for m in (1, 2, 3)]
    weights = call(
        fetched,
        [array(2, features, features)] * 2,
        1,
        [HBM] * 2,
        *(in_hbm(w) for w in together(keep_proj, sibling_proj, sent[0])[:2]),
        scratch=[pltpu.SemaphoreType.DMA((2,))],
    )
    y0, y1 = call(second_level, [part] * 2, 1, [VMEM] * 4, x[0], x[1], *weights)
    if few:
        x_mine, y_other, _ = together(*near, sent[0])
        (pack_near,) = call(packed, [array(2 * depth, features)], 1, [VMEM] * 2, x_mine, y_other)
        pack_far = swapped(pack_near, 1, "blk")
        d_mine, d_other = swapped(after(x_mine, y0), 4), swapped(after(y_other, y0), 2)
    done = call(third_level, [part] * 4, (1 << 34), [VMEM] * 6, x[2], x[3], y0, y1, *weights)
    back = [done[0]] + [swapped(done[m], 2 * m) for m in (1, 2, 3)]
    if not few:
        current = jnp.zeros((rows, features), jnp.bfloat16)
        for m in range(4):
            current = lax.dynamic_update_slice_in_dim(current, back[m], ((me[0] // 2 % 4) ^ m) * quarter, 0)
        return routed(current, owners, jnp.where(z[0] % 2 == 0, jnp.concatenate([mine, other]), jnp.concatenate([other, mine])))
    pieces = [mine, other, pack_near, pack_far, d_mine, d_other]
    (pack,) = call(packed, [array(8 * depth, features)], 1, [VMEM] * 6, *together(*pieces, done[0])[:6])
    matrices = [pack, swapped(pack, 1)]
    returned = [back[m] for m in (1,)]
    *returned, = call(passed, [part] * len(returned), 1 << 36, [VMEM] * len(returned), *returned)
    for m, rows_back in zip((1,), returned):
        back[m] = rows_back
    (relative,) = call(
        named, [(jax.ShapeDtypeStruct((rows, 128), jnp.int32), VMEM)], 1, [SMEM, VMEM], me, after(owners.reshape(-1, 128), done[0])
    )
    out = None
    for blocks in ((0, 1), (2, 3)):
        extra = [] if out is None else [out]
        n_block = len(blocks)
        (out,) = call(
            functools.partial(couple, blocks),
            [whole],
            8 * n_block * block_flops,
            [SMEM] * 2 + [VMEM] * (1 + n_block + len(matrices)) + [HBM] * len(extra),
            me,
            z,
            relative,
            *(back[m] for m in blocks),
            *matrices,
            *extra,
            scratch=[pltpu.VMEM((n_block * quarter, features), jnp.bfloat16), pltpu.SemaphoreType.DMA((2, n_block))],
            aliases={3 + n_block + len(matrices): 0} if extra else None,
        )
    return out


def solution(mesh):
    in_specs = (
        P(("leaf", "blk"), None),
        P(("leaf", "blk"), None),
        P(),
        P(),
        P("leaf", None, None),
        P("leaf", None, None),
    )
    out_specs = P(("leaf", "blk"), None)
    return jax.shard_map(local, mesh=mesh, in_specs=in_specs, out_specs=out_specs, check_vma=False)
```

```python
import functools
import jax
import jax.numpy as jnp
from jax import lax
from jax.experimental import pallas as pl
from jax.experimental.pallas import tpu as pltpu
from jax.sharding import PartitionSpec as P

BS = 64
EPSILON = 1e-06
PLACES = (0, 1), (2, 4), (5, 3), (6, 7)
VMEM = pl.BlockSpec(memory_space=pltpu.VMEM)
SMEM = pl.BlockSpec(memory_space=pltpu.SMEM)
HBM = pl.BlockSpec(memory_space=pltpu.HBM)


def swapped(value, mask, axis="leaf"):
    pairs = [(source, source ^ mask) for source in range(lax.axis_size(axis))]
    return lax.ppermute(value, axis, pairs)


def in_hbm(value):
    return pltpu.with_memory_space_constraint(value, pltpu.HBM)


def together(*values):
    return lax.optimization_barrier(values)


def after(value, *others):
    return lax.optimization_barrier((value, *others))[0]


def mixed(own, sibling, keep, cross):
    combined = jnp.dot(own, keep, preferred_element_type=jnp.float32)
    return normal(combined + jnp.dot(sibling, cross, preferred_element_type=jnp.float32))


def normal(combined):
    scale_rows = lax.rsqrt(jnp.mean(combined * combined, axis=1, keepdims=True) + EPSILON)
    return (combined * scale_rows).astype(jnp.bfloat16)


def call(body, outs, flops, specs, *args, scratch=(), aliases=None):
    return pl.pallas_call(
        body,
        out_shape=[shape for shape, _ in outs],
        in_specs=specs,
        out_specs=[spec for _, spec in outs],
        scratch_shapes=list(scratch),
        input_output_aliases=aliases or {},
        cost_estimate=pl.CostEstimate(flops=flops, bytes_accessed=flops // 512, transcendentals=0),
        compiler_params=pltpu.CompilerParams(vmem_limit_bytes=24 << 20),
    )(*args)


def block_rows(me, m, size):
    return pl.ds(pl.multiple_of((((me[0] >> 1) & 3) ^ m) * size, size), size)


def first_level(me, sibling, interface, keep, cross, *rest):
    outs, (own, keep_here, cross_here, sems) = rest[:4], rest[4:]
    size = outs[0].shape[0]
    order = (1, 2, 3, 0)
    loads = [
        pltpu.make_async_copy(cross.at[0], cross_here, sems.at[5]),
        pltpu.make_async_copy(keep.at[0], keep_here, sems.at[4]),
    ]
    for m in order:
        rows = block_rows(me, m, size)
        loads.append(pltpu.make_async_copy(interface.at[rows], own.at[rows], sems.at[m]))
    for load in loads:
        load.start()
    loads[0].wait()
    terms = []
    for m in order:
        terms.append(jnp.dot(sibling[block_rows(me, m, size), :], cross_here[...], preferred_element_type=jnp.float32))
    loads[1].wait()
    for m, load, term in zip(order, loads[2:], terms):
        load.wait()
        rows = block_rows(me, m, size)
        outs[m][...] = normal(jnp.dot(own[rows, :], keep_here[...], preferred_element_type=jnp.float32) + term)


def second_level(x0, x1, keep, cross, *outs):
    y = mixed(x0[...], x1[...], keep[0], cross[0]), mixed(x1[...], x0[...], keep[0], cross[0])
    for m in range(2):
        outs[m][...] = jnp.dot(y[m], keep[1], preferred_element_type=jnp.float32)
        outs[m + 2][...] = jnp.dot(y[m], cross[1], preferred_element_type=jnp.float32)


def third_level(x2, x3, term0, term1, term2, term3, keep, cross, *outs):
    y2 = mixed(x2[...], x3[...], keep[0], cross[0])
    y3 = mixed(x3[...], x2[...], keep[0], cross[0])
    outs[1][...] = normal(term1[...] + jnp.dot(y3, cross[1], preferred_element_type=jnp.float32))
    outs[2][...] = normal(jnp.dot(y2, keep[1], preferred_element_type=jnp.float32) + term2[...])
    outs[3][...] = normal(jnp.dot(y3, keep[1], preferred_element_type=jnp.float32) + term3[...])
    outs[0][...] = normal(term0[...] + jnp.dot(y2, cross[1], preferred_element_type=jnp.float32))


def masked_coupling(z, coupling, pattern, part, rest, held, shown, sems):
    loads = [pltpu.make_async_copy(pattern, shown, sems.at[0]), pltpu.make_async_copy(coupling, held, sems.at[1])]
    for load in loads:
        load.start()
    for load in loads:
        load.wait()
    for i in range(shown.shape[1]):
        row = jnp.concatenate(
            [jnp.full((BS, BS), shown[0, i, j], jnp.int32) for j in range(shown.shape[2])], axis=1
        )
        block = held[0, i * BS : (i + 1) * BS, :]
        held[0, i * BS : (i + 1) * BS, :] = jnp.where(row != 0, block, jnp.zeros_like(block))
    part[...] = held[0, half_rows(z, 0, part.shape[0]), :]
    rest[...] = held[0, half_rows(z, 1, part.shape[0]), :]


def half_rows(z, other, depth):
    return pl.ds(pl.multiple_of(((z[0] & 1) ^ other) * depth, depth), depth)


def packed(*refs):
    *parts, out = refs
    at = 0
    for part in parts:
        out[at : at + part.shape[0], :] = part[...]
        at += part.shape[0]


def named(me, owners, out):
    lanes = owners.shape[1]
    groups = owners.shape[0] // 4
    diagonal = lax.broadcasted_iota(jnp.int32, (lanes, lanes), 0) == lax.broadcasted_iota(jnp.int32, (lanes, lanes), 1)
    for m in range(4):
        block = owners[pl.ds((((me[0] >> 1) & 3) ^ m) * groups, groups), :] ^ me[0]
        for i in range(groups):
            column = jnp.sum(jnp.where(diagonal, block[i : i + 1, :], 0), axis=1, keepdims=True)
            at = (m * groups + i) * lanes
            out[at : at + lanes, :] = jnp.broadcast_to(column, (lanes, lanes))


def couple(blocks, me, z, owners, *rest):
    n_block = len(blocks)
    xs, packs, (out, held, sems) = rest[:n_block], rest[n_block : n_block + 2], rest[-3:]
    size, features = xs[0].shape
    depth = features // 2
    wide = jnp.concatenate([owners[m * size : (m + 1) * size, :] for m in blocks], axis=0)
    relative = jnp.concatenate([wide] * (depth // wide.shape[1]), axis=1)
    parts = [half_rows(z, other, depth) for other in range(2)]
    values = [jnp.concatenate([x[:, part] for x in xs], axis=0) for part in parts]
    copies = []
    for n in range(2):
        columns = slice(n * depth, (n + 1) * depth)
        total = jnp.zeros((n_block * size, depth), jnp.float32)
        for r in range(8):
            halves = [packs[r % 2][at * depth : (at + 1) * depth, columns] for at in PLACES[r // 2]]
            each = [jnp.dot(v, half, preferred_element_type=jnp.float32) for v, half in zip(values, halves)]
            total = jnp.where(relative == r, each[0] + each[1], total)
        held[:, columns] = total.astype(jnp.bfloat16)
        for i, m in enumerate(blocks):
            to = out.at[block_rows(me, m, size), columns]
            copies.append(pltpu.make_async_copy(held.at[i * size : (i + 1) * size, columns], to, sems.at[n, i]))
            copies[-1].start()
    for copy in copies:
        copy.wait()


def passed(*refs):
    count = len(refs) // 2
    for value, out in zip(refs[:count], refs[count:]):
        out[...] = value[...]


def fetched(keep, cross, keep_here, cross_here, sems):
    loads = [
        pltpu.make_async_copy(keep.at[1:], keep_here, sems.at[0]),
        pltpu.make_async_copy(cross.at[1:], cross_here, sems.at[1]),
    ]
    for load in loads:
        load.start()
    for load in loads:
        load.wait()


def routed(current, owners, dense):
    row_count, features = current.shape
    leaves = lax.axis_size("leaf")
    capacity = 2 * row_count // leaves
    target = owners[:, 0]
    onehot = (target[:, None] == jnp.arange(leaves, dtype=jnp.int32)[None, :]).astype(jnp.int32)
    slot_index = jnp.sum(jnp.cumsum(onehot, axis=0) * onehot, axis=1) - 1
    position = target * capacity + slot_index
    outgoing = jnp.zeros((leaves * capacity, features), jnp.bfloat16).at[position].set(current)
    sectioned = outgoing.reshape(leaves, capacity, features)
    arrived = lax.all_to_all(sectioned, "leaf", split_axis=0, concat_axis=0, tiled=True)
    product = jnp.einsum("...m,mn->...n", arrived, dense, preferred_element_type=jnp.float32)
    result = product.astype(jnp.bfloat16)
    returned = lax.all_to_all(result, "leaf", split_axis=0, concat_axis=0, tiled=True)
    return returned.reshape(leaves * capacity, features)[position]


def local(interface, owners, keep_proj, sibling_proj, coupling, pattern):
    rows, features = interface.shape
    leaves = lax.axis_size("leaf")
    me = lax.axis_index("leaf").astype(jnp.int32).reshape(1)
    z = lax.axis_index("blk").astype(jnp.int32).reshape(1)
    few = leaves == 8 and lax.axis_size("blk") % 2 == 0
    quarter = rows // 4
    depth = features // 2
    block_flops = 2 * quarter * features * features

    def array(*shape, space=VMEM):
        return jax.ShapeDtypeStruct(shape, jnp.bfloat16), space

    part = array(quarter, features)
    whole = array(rows, features, space=HBM)
    matrix = array(features, features)
    weights = in_hbm(keep_proj), in_hbm(sibling_proj)

    sibling = swapped(interface, 1)
    mine, other = call(
        masked_coupling,
        [array(depth, features)] * 2,
        1,
        [SMEM] + [HBM] * 2,
        z,
        in_hbm(coupling),
        in_hbm(pattern),
        scratch=[
            pltpu.VMEM(coupling.shape, coupling.dtype),
            pltpu.SMEM(pattern.shape, pattern.dtype),
            pltpu.SemaphoreType.DMA((2,)),
        ],
    )
    if few:
        near = swapped(mine, 2), swapped(other, 4)
    sent = call(
        first_level,
        [part] * 4,
        4 * block_flops,
        [SMEM, VMEM] + [HBM] * 3,
        me,
        sibling,
        in_hbm(interface),
        *weights,
        scratch=[pltpu.VMEM((rows, features), jnp.bfloat16)]
        + [pltpu.VMEM((features, features), jnp.bfloat16)] * 2
        + [pltpu.SemaphoreType.DMA((6,))],
    )
    x = [sent[0]] + [swapped(sent[m], 2 * m) for m in (1, 2, 3)]
    weights = call(
        fetched,
        [array(2, features, features)] * 2,
        1,
        [HBM] * 2,
        *(in_hbm(w) for w in together(keep_proj, sibling_proj, sent[0])[:2]),
        scratch=[pltpu.SemaphoreType.DMA((2,))],
    )
    term = jax.ShapeDtypeStruct((quarter, features), jnp.float32), VMEM
    terms = call(second_level, [term] * 4, 1, [VMEM] * 4, x[0], x[1], *weights)
    if few:
        x_mine, y_other, _ = together(*near, sent[0])
        (pack_near,) = call(packed, [array(2 * depth, features)], 1, [VMEM] * 2, x_mine, y_other)
        pack_far = swapped(pack_near, 1, "blk")
        d_mine, d_other = swapped(after(x_mine, x[1]), 4), swapped(after(y_other, x[1]), 2)
    done = call(third_level, [part] * 4, (1 << 34), [VMEM] * 8, x[2], x[3], *terms, *weights)
    back = [done[0]] + [swapped(done[m], 2 * m) for m in (1, 2, 3)]
    if not few:
        current = jnp.zeros((rows, features), jnp.bfloat16)
        for m in range(4):
            current = lax.dynamic_update_slice_in_dim(current, back[m], ((me[0] // 2 % 4) ^ m) * quarter, 0)
        return routed(current, owners, jnp.where(z[0] % 2 == 0, jnp.concatenate([mine, other]), jnp.concatenate([other, mine])))
    pieces = [mine, other, pack_near, pack_far, d_mine, d_other]
    (pack,) = call(packed, [array(8 * depth, features)], 1, [VMEM] * 6, *together(*pieces, done[0])[:6])
    matrices = [pack, swapped(pack, 1)]
    returned = [back[m] for m in (1,)]
    *returned, = call(passed, [part] * len(returned), 1 << 35, [VMEM] * len(returned), *returned)
    for m, rows_back in zip((1,), returned):
        back[m] = rows_back
    (relative,) = call(
        named, [(jax.ShapeDtypeStruct((rows, 128), jnp.int32), VMEM)], 1, [SMEM, VMEM], me, after(owners.reshape(-1, 128), done[0])
    )
    out = None
    for blocks in ((0, 1), (2, 3)):
        extra = [] if out is None else [out]
        n_block = len(blocks)
        (out,) = call(
            functools.partial(couple, blocks),
            [whole],
            8 * n_block * block_flops,
            [SMEM] * 2 + [VMEM] * (1 + n_block + len(matrices)) + [HBM] * len(extra),
            me,
            z,
            relative,
            *(back[m] for m in blocks),
            *matrices,
            *extra,
            scratch=[pltpu.VMEM((n_block * quarter, features), jnp.bfloat16), pltpu.SemaphoreType.DMA((2, n_block))],
            aliases={3 + n_block + len(matrices): 0} if extra else None,
        )
    return out


def solution(mesh):
    in_specs = (
        P(("leaf", "blk"), None),
        P(("leaf", "blk"), None),
        P(),
        P(),
        P("leaf", None, None),
        P("leaf", None, None),
    )
    out_specs = P(("leaf", "blk"), None)
    return jax.shard_map(local, mesh=mesh, in_specs=in_specs, out_specs=out_specs, check_vma=False)
```

```python
import functools
import jax
import jax.numpy as jnp
from jax import lax
from jax.experimental import pallas as pl
from jax.experimental.pallas import tpu as pltpu
from jax.sharding import PartitionSpec as P

BS = 64
EPSILON = 1e-06
PLACES = (0, 1), (2, 4), (5, 3), (6, 7)
VMEM = pl.BlockSpec(memory_space=pltpu.VMEM)
SMEM = pl.BlockSpec(memory_space=pltpu.SMEM)
HBM = pl.BlockSpec(memory_space=pltpu.HBM)


def swapped(value, mask, axis="leaf"):
    pairs = [(source, source ^ mask) for source in range(lax.axis_size(axis))]
    return lax.ppermute(value, axis, pairs)


def in_hbm(value):
    return pltpu.with_memory_space_constraint(value, pltpu.HBM)


def together(*values):
    return lax.optimization_barrier(values)


def after(value, *others):
    return lax.optimization_barrier((value, *others))[0]


def mixed(own, sibling, keep, cross):
    combined = jnp.dot(own, keep, preferred_element_type=jnp.float32)
    return normal(combined + jnp.dot(sibling, cross, preferred_element_type=jnp.float32))


def normal(combined):
    scale_rows = lax.rsqrt(jnp.mean(combined * combined, axis=1, keepdims=True) + EPSILON)
    return (combined * scale_rows).astype(jnp.bfloat16)


def call(body, outs, flops, specs, *args, scratch=(), aliases=None):
    return pl.pallas_call(
        body,
        out_shape=[shape for shape, _ in outs],
        in_specs=specs,
        out_specs=[spec for _, spec in outs],
        scratch_shapes=list(scratch),
        input_output_aliases=aliases or {},
        cost_estimate=pl.CostEstimate(flops=flops, bytes_accessed=flops // 512, transcendentals=0),
        compiler_params=pltpu.CompilerParams(vmem_limit_bytes=24 << 20),
    )(*args)


def block_rows(me, m, size):
    return pl.ds(pl.multiple_of((((me[0] >> 1) & 3) ^ m) * size, size), size)


def first_level(me, sibling, interface, keep, cross, *rest):
    outs, (own, keep_here, cross_here, sems) = rest[:4], rest[4:]
    size = outs[0].shape[0]
    order = (1, 2, 3, 0)
    loads = [
        pltpu.make_async_copy(cross.at[0], cross_here, sems.at[5]),
        pltpu.make_async_copy(keep.at[0], keep_here, sems.at[4]),
    ]
    for m in order:
        rows = block_rows(me, m, size)
        loads.append(pltpu.make_async_copy(interface.at[rows], own.at[rows], sems.at[m]))
    for load in loads:
        load.start()
    loads[0].wait()
    terms = []
    for m in order:
        terms.append(jnp.dot(sibling[block_rows(me, m, size), :], cross_here[...], preferred_element_type=jnp.float32))
    loads[1].wait()
    for m, load, term in zip(order, loads[2:], terms):
        load.wait()
        rows = block_rows(me, m, size)
        outs[m][...] = normal(jnp.dot(own[rows, :], keep_here[...], preferred_element_type=jnp.float32) + term)


def second_level(x0, x1, keep, cross, *outs):
    y = mixed(x0[...], x1[...], keep[0], cross[0]), mixed(x1[...], x0[...], keep[0], cross[0])
    for m in range(2):
        outs[m][...] = jnp.dot(y[m], keep[1], preferred_element_type=jnp.float32)
        outs[m + 2][...] = jnp.dot(y[m], cross[1], preferred_element_type=jnp.float32)


def third_level(x2, x3, term0, term1, term2, term3, keep, cross, *outs):
    y2 = mixed(x2[...], x3[...], keep[0], cross[0])
    y3 = mixed(x3[...], x2[...], keep[0], cross[0])
    outs[1][...] = normal(term1[...] + jnp.dot(y3, cross[1], preferred_element_type=jnp.float32))
    outs[2][...] = normal(jnp.dot(y2, keep[1], preferred_element_type=jnp.float32) + term2[...])
    outs[3][...] = normal(jnp.dot(y3, keep[1], preferred_element_type=jnp.float32) + term3[...])
    outs[0][...] = normal(term0[...] + jnp.dot(y2, cross[1], preferred_element_type=jnp.float32))


def masked_coupling(z, coupling, pattern, part, rest, held, shown, sems):
    loads = [pltpu.make_async_copy(pattern, shown, sems.at[0]), pltpu.make_async_copy(coupling, held, sems.at[1])]
    for load in loads:
        load.start()
    for load in loads:
        load.wait()
    for i in range(shown.shape[1]):
        row = jnp.concatenate(
            [jnp.full((BS, BS), shown[0, i, j], jnp.int32) for j in range(shown.shape[2])], axis=1
        )
        block = held[0, i * BS : (i + 1) * BS, :]
        held[0, i * BS : (i + 1) * BS, :] = jnp.where(row != 0, block, jnp.zeros_like(block))
    part[...] = held[0, half_rows(z, 0, part.shape[0]), :]
    rest[...] = held[0, half_rows(z, 1, part.shape[0]), :]


def half_rows(z, other, depth):
    return pl.ds(pl.multiple_of(((z[0] & 1) ^ other) * depth, depth), depth)


def packed(*refs):
    *parts, out = refs
    at = 0
    for part in parts:
        out[at : at + part.shape[0], :] = part[...]
        at += part.shape[0]


def named(me, owners, out):
    lanes = owners.shape[1]
    groups = owners.shape[0] // 4
    diagonal = lax.broadcasted_iota(jnp.int32, (lanes, lanes), 0) == lax.broadcasted_iota(jnp.int32, (lanes, lanes), 1)
    for m in range(4):
        block = owners[pl.ds((((me[0] >> 1) & 3) ^ m) * groups, groups), :] ^ me[0]
        for i in range(groups):
            column = jnp.sum(jnp.where(diagonal, block[i : i + 1, :], 0), axis=1, keepdims=True)
            at = (m * groups + i) * lanes
            out[at : at + lanes, :] = jnp.broadcast_to(column, (lanes, lanes))


def couple(blocks, me, z, owners, *rest):
    n_block = len(blocks)
    xs, packs, (out, held, sems) = rest[:n_block], rest[n_block : n_block + 2], rest[-3:]
    size, features = xs[0].shape
    depth = features // 2
    wide = jnp.concatenate([owners[m * size : (m + 1) * size, :] for m in blocks], axis=0)
    relative = jnp.concatenate([wide] * (depth // wide.shape[1]), axis=1)
    parts = [half_rows(z, other, depth) for other in range(2)]
    values = [jnp.concatenate([x[:, part] for x in xs], axis=0) for part in parts]
    copies = []
    for n in range(2):
        columns = slice(n * depth, (n + 1) * depth)
        total = jnp.zeros((n_block * size, depth), jnp.float32)
        for r in range(8):
            halves = [packs[r % 2][at * depth : (at + 1) * depth, columns] for at in PLACES[r // 2]]
            each = [jnp.dot(v, half, preferred_element_type=jnp.float32) for v, half in zip(values, halves)]
            total = jnp.where(relative == r, each[0] + each[1], total)
        held[:, columns] = total.astype(jnp.bfloat16)
        for i, m in enumerate(blocks):
            to = out.at[block_rows(me, m, size), columns]
            copies.append(pltpu.make_async_copy(held.at[i * size : (i + 1) * size, columns], to, sems.at[n, i]))
            copies[-1].start()
    for copy in copies:
        copy.wait()


def passed(*refs):
    count = len(refs) // 2
    for value, out in zip(refs[:count], refs[count:]):
        out[...] = value[...]


def fetched(keep, cross, keep_here, cross_here, sems):
    loads = [
        pltpu.make_async_copy(keep.at[1:], keep_here, sems.at[0]),
        pltpu.make_async_copy(cross.at[1:], cross_here, sems.at[1]),
    ]
    for load in loads:
        load.start()
    for load in loads:
        load.wait()


def routed(current, owners, dense):
    row_count, features = current.shape
    leaves = lax.axis_size("leaf")
    capacity = 2 * row_count // leaves
    target = owners[:, 0]
    onehot = (target[:, None] == jnp.arange(leaves, dtype=jnp.int32)[None, :]).astype(jnp.int32)
    slot_index = jnp.sum(jnp.cumsum(onehot, axis=0) * onehot, axis=1) - 1
    position = target * capacity + slot_index
    outgoing = jnp.zeros((leaves * capacity, features), jnp.bfloat16).at[position].set(current)
    sectioned = outgoing.reshape(leaves, capacity, features)
    arrived = lax.all_to_all(sectioned, "leaf", split_axis=0, concat_axis=0, tiled=True)
    product = jnp.einsum("...m,mn->...n", arrived, dense, preferred_element_type=jnp.float32)
    result = product.astype(jnp.bfloat16)
    returned = lax.all_to_all(result, "leaf", split_axis=0, concat_axis=0, tiled=True)
    return returned.reshape(leaves * capacity, features)[position]


def local(interface, owners, keep_proj, sibling_proj, coupling, pattern):
    rows, features = interface.shape
    leaves = lax.axis_size("leaf")
    me = lax.axis_index("leaf").astype(jnp.int32).reshape(1)
    z = lax.axis_index("blk").astype(jnp.int32).reshape(1)
    few = leaves == 8 and lax.axis_size("blk") % 2 == 0
    quarter = rows // 4
    depth = features // 2
    block_flops = 2 * quarter * features * features

    def array(*shape, space=VMEM):
        return jax.ShapeDtypeStruct(shape, jnp.bfloat16), space

    part = array(quarter, features)
    whole = array(rows, features, space=HBM)
    matrix = array(features, features)
    weights = in_hbm(keep_proj), in_hbm(sibling_proj)

    sibling = swapped(interface, 1)
    mine, other = call(
        masked_coupling,
        [array(depth, features)] * 2,
        1,
        [SMEM] + [HBM] * 2,
        z,
        in_hbm(coupling),
        in_hbm(pattern),
        scratch=[
            pltpu.VMEM(coupling.shape, coupling.dtype),
            pltpu.SMEM(pattern.shape, pattern.dtype),
            pltpu.SemaphoreType.DMA((2,)),
        ],
    )
    if few:
        near = swapped(mine, 2), swapped(other, 4)
    sent = call(
        first_level,
        [part] * 4,
        4 * block_flops,
        [SMEM, VMEM] + [HBM] * 3,
        me,
        sibling,
        in_hbm(interface),
        *weights,
        scratch=[pltpu.VMEM((rows, features), jnp.bfloat16)]
        + [pltpu.VMEM((features, features), jnp.bfloat16)] * 2
        + [pltpu.SemaphoreType.DMA((6,))],
    )
    x = [sent[0]] + [swapped(sent[m], 2 * m) for m in (1, 2, 3)]
    weights = call(
        fetched,
        [array(2, features, features)] * 2,
        1,
        [HBM] * 2,
        *(in_hbm(w) for w in together(keep_proj, sibling_proj, sent[0])[:2]),
        scratch=[pltpu.SemaphoreType.DMA((2,))],
    )
    term = jax.ShapeDtypeStruct((quarter, features), jnp.float32), VMEM
    terms = call(second_level, [term] * 4, 1, [VMEM] * 4, x[0], x[1], *weights)
    if few:
        x_mine, y_other, _ = together(*near, sent[0])
        (pack_near,) = call(packed, [array(2 * depth, features)], 1, [VMEM] * 2, x_mine, y_other)
        pack_far = swapped(pack_near, 1, "blk")
        d_mine, d_other = swapped(after(x_mine, x[1]), 4), swapped(after(y_other, terms[0]), 2)
    done = call(third_level, [part] * 4, (1 << 34), [VMEM] * 8, x[2], x[3], *terms, *weights)
    back = [done[0]] + [swapped(done[m], 2 * m) for m in (1, 2, 3)]
    if not few:
        current = jnp.zeros((rows, features), jnp.bfloat16)
        for m in range(4):
            current = lax.dynamic_update_slice_in_dim(current, back[m], ((me[0] // 2 % 4) ^ m) * quarter, 0)
        return routed(current, owners, jnp.where(z[0] % 2 == 0, jnp.concatenate([mine, other]), jnp.concatenate([other, mine])))
    pieces = [mine, other, pack_near, pack_far, d_mine, d_other]
    (pack,) = call(packed, [array(8 * depth, features)], 1, [VMEM] * 6, *together(*pieces, done[0])[:6])
    matrices = [pack, swapped(pack, 1)]
    returned = [back[m] for m in (1,)]
    *returned, = call(passed, [part] * len(returned), 1 << 35, [VMEM] * len(returned), *returned)
    for m, rows_back in zip((1,), returned):
        back[m] = rows_back
    (relative,) = call(
        named, [(jax.ShapeDtypeStruct((rows, 128), jnp.int32), VMEM)], 1, [SMEM, VMEM], me, after(owners.reshape(-1, 128), done[0])
    )
    out = None
    for blocks in ((0, 1), (2, 3)):
        extra = [] if out is None else [out]
        n_block = len(blocks)
        (out,) = call(
            functools.partial(couple, blocks),
            [whole],
            8 * n_block * block_flops,
            [SMEM] * 2 + [VMEM] * (1 + n_block + len(matrices)) + [HBM] * len(extra),
            me,
            z,
            relative,
            *(back[m] for m in blocks),
            *matrices,
            *extra,
            scratch=[pltpu.VMEM((n_block * quarter, features), jnp.bfloat16), pltpu.SemaphoreType.DMA((2, n_block))],
            aliases={3 + n_block + len(matrices): 0} if extra else None,
        )
    return out


def solution(mesh):
    in_specs = (
        P(("leaf", "blk"), None),
        P(("leaf", "blk"), None),
        P(),
        P(),
        P("leaf", None, None),
        P("leaf", None, None),
    )
    out_specs = P(("leaf", "blk"), None)
    return jax.shard_map(local, mesh=mesh, in_specs=in_specs, out_specs=out_specs, check_vma=False)
```
